32 devices in a mesh: scene: 2 (over y), pts: 4 (over z), view: 2 (over x), head: 2 (over core).
Axes of the slice: x: 2, y: 2, z: 4, core: 2. Of those that a mesh axis runs over, the one named last changes fastest.
Arguments:
- queries: bfloat16 [2048, 1024], P(('scene', 'pts'), 'head'), parts along dimension 0, may hold values from -8 to 8
- key_tiles: bfloat16 [128, 16, 1024], P(('scene', 'pts', 'view'), None, 'head'), parts along dimension 0, may hold values from -4 to 4
- value_tiles: bfloat16 [128, 16, 1024], P(('scene', 'pts', 'view'), None, 'head'), parts along dimension 0, may hold values from -6 to 6
- visible: int32 [16, 32], P(('scene', 'pts'), 'view'), parts along dimension 0, may hold values from 0 to 63, as said below
- destination: int32 [2048], P(('scene', 'pts')), parts along dimension 0, may hold values from 0 to 1023, as said below
- d_out: bfloat16 [2048, 1024], P(('scene', 'pts'), 'head'), parts along dimension 0, may hold values from -6 to 6
Outputs:
- attended: bfloat16 [2048, 1024], P(('scene', 'pts'), 'head'), parts along dimension 0
- d_queries: bfloat16 [2048, 1024], P(('scene', 'pts'), 'head'), parts along dimension 0
- d_keys: bfloat16 [128, 16, 1024], P(('scene', 'pts', 'view'), None, 'head'), parts along dimension 0
- d_values: bfloat16 [128, 16, 1024], P(('scene', 'pts', 'view'), None, 'head'), parts along dimension 0
The draws below stay inside these ranges and needn't reach their ends.
There are 2 independent parts, one for each index of `scene`. The reference program is written for one: setup_inputs(seed, part) draws one part's arguments, and reference() takes and returns one part's arrays. A program takes and returns all parts, laid end to end along the dimension named above; each array names one. Nothing has to cross between parts.
Inputs may be any that keep to these rules, and one draw needn't show every extreme that they name: `visible`: the 16 ids that one query block lists for view group v are distinct tiles held by devices of view index v. The lists of the query blocks of one pts index for one view group name exactly 32 distinct tiles, at most 8 of them held by any one device, and exactly 8 held by some device. `destination`: A permutation of the 1024 rows. The rows of each pts index go to the rows of every pts index, exactly 64 to each.
All inputs are finite; a program needn't handle non-finite values.
Results may differ from the reference program's by a relative error of at most 0.017.
Values may be sent and summed in bfloat16 or wider, within the bound.
A program may use at most 64 MiB of HBM per device.

```python
import jax
import jax.numpy as jnp
from jax import lax

HEADS = 16
DH = 64
QBLOCK = 128
TILE = 16
NVIS = 16
DIST = 32
QB_DEV = 2
KV_DEV = 8
CAP = 8
P_DEV = 256
NPTS = 1024
NQB = 8
HD = 1024
VIS = 32
KVTILES = 64
N_PTS = 4
N_VIEW = 2


def draw_queries(key, part):
    return jnp.clip(jax.random.normal(jax.random.fold_in(key, 11), (NPTS, HD), jnp.float32), -4.0, 4.0).astype(jnp.bfloat16)


def draw_key_tiles(key, part):
    shape_all = (KVTILES, TILE, HD)
    return jnp.clip(jax.random.normal(jax.random.fold_in(key, 12), shape_all, jnp.float32), -4.0, 4.0).astype(jnp.bfloat16)


def device_lists(device_key, view_index):
    slots_total = N_PTS * CAP
    shuffled = jax.random.permutation(jax.random.fold_in(device_key, 1), slots_total)
    full_owner = jax.random.randint(jax.random.fold_in(device_key, 2), (), 0, N_PTS)
    sort_key = jnp.where(shuffled // CAP == full_owner, -1, jnp.arange(slots_total))
    ordered = shuffled[jnp.argsort(sort_key, stable=True)]
    chosen = ordered[:DIST]
    owner_of = chosen // CAP
    copy_of = chosen % CAP
    base_ids = jax.random.randint(jax.random.fold_in(device_key, 3), (N_PTS,), 0, KV_DEV)
    local_id = (base_ids[owner_of] + copy_of) % KV_DEV
    tile_ids = (owner_of * N_VIEW + view_index) * KV_DEV + local_id
    repeats = -(-(QB_DEV * NVIS) // DIST)
    rounds_list = []
    for round_number in range(repeats):
        mixing = jax.random.permutation(jax.random.fold_in(device_key, 100 + round_number), DIST)
        rounds_list.append(tile_ids[mixing])
    joined = jnp.concatenate(rounds_list)
    return joined[:QB_DEV * NVIS].reshape(QB_DEV, NVIS)


def draw_visible(key, part):

    def one_device(device_number):
        device_key = jax.random.fold_in(key, device_number)
        return device_lists(device_key, device_number % N_VIEW)
    lists_all = jax.vmap(one_device)(jnp.arange(N_PTS * N_VIEW))
    lists_all = lists_all.reshape(N_PTS, N_VIEW, QB_DEV, NVIS)
    lists_all = jnp.transpose(lists_all, (0, 2, 1, 3))
    return lists_all.reshape(NQB, VIS).astype(jnp.int32)


def draw_destination(key, part):
    per_peer = P_DEV // N_PTS

    def sender_order(sender_number):
        return jax.random.permutation(jax.random.fold_in(key, sender_number), P_DEV)

    def receiver_order(receiver_number):
        return jax.random.permutation(jax.random.fold_in(key, N_PTS + receiver_number), P_DEV)
    sent_rows = jax.vmap(sender_order)(jnp.arange(N_PTS))
    arrange = jax.vmap(receiver_order)(jnp.arange(N_PTS))
    sequence = jnp.arange(P_DEV)
    target = jnp.broadcast_to((sequence // per_peer)[None, :], (N_PTS, P_DEV))
    within = jnp.arange(N_PTS)[:, None] * per_peer + (sequence % per_peer)[None, :]
    dest_seq = target * P_DEV + arrange[target, within]
    inverse = jnp.argsort(sent_rows, axis=1)
    by_row = jnp.take_along_axis(dest_seq, inverse, axis=1)
    return by_row.reshape(-1).astype(jnp.int32)


def shard_levels(rng, extent, cuts, low, high):
    level = 1.0
    for axis_at, shards_of in cuts:
        draws = jax.random.uniform(jax.random.fold_in(jax.random.fold_in(rng, 6), axis_at), (shards_of,), jnp.float32, low / len(cuts), high / len(cuts))
        level = level * jnp.repeat(jnp.exp(draws), extent[axis_at] // shards_of).reshape((-1,) + (1,) * (len(extent) - 1 - axis_at))
    return level


def centred(stream_key, extent, spread, most, cuts=(), held_as=jnp.bfloat16):
    entries = jax.random.normal(stream_key, extent, jnp.float32) * spread
    if len(cuts) > 0:
        entries = shard_levels(stream_key, extent, cuts, -0.22, 0.18) * entries
    return jnp.clip(entries, min=-most, max=most).astype(held_as)


def setup_inputs(seed: int = 0, part: int = 0) -> dict:
    arg_keys = jax.random.split(jax.random.key(seed), 7)
    part_splits = jax.random.split(jax.random.fold_in(arg_keys[6], part), 7)
    return {
        "queries": draw_queries(jax.random.fold_in(jax.random.fold_in(arg_keys[6], part), 71), part),
        "key_tiles": draw_key_tiles(jax.random.fold_in(jax.random.fold_in(arg_keys[6], part), 71), part),
        "value_tiles": centred(part_splits[2], (KVTILES, TILE, HD), 1.0, 6.0, ((0, 8), (2, 2))),
        "visible": draw_visible(jax.random.fold_in(jax.random.fold_in(arg_keys[6], part), 71), part),
        "destination": draw_destination(jax.random.fold_in(jax.random.fold_in(arg_keys[6], part), 71), part),
        "d_out": centred(part_splits[5], (NPTS, HD), 1.0, 6.0, ((0, 4), (1, 2))),
    }


HIGHEST = lax.Precision.HIGHEST


def rounded(values):
    return lax.optimization_barrier(values.astype(jnp.bfloat16)).astype(jnp.float32)


def device_pass(key_tiles, value_tiles, queries, visible, d_out):
    score_scale = DH ** -0.5
    query_f = queries.reshape(QB_DEV, QBLOCK, HEADS, DH).astype(jnp.float32)
    grad_f = d_out.reshape(QB_DEV, QBLOCK, HEADS, DH).astype(jnp.float32)
    tile_ids = visible.reshape(QB_DEV, N_VIEW, NVIS)
    key_f = key_tiles[tile_ids].reshape(QB_DEV, N_VIEW, NVIS * TILE, HEADS, DH).astype(jnp.float32)
    value_f = value_tiles[tile_ids].reshape(QB_DEV, N_VIEW, NVIS * TILE, HEADS, DH).astype(jnp.float32)
    scores = jnp.einsum("bqhd,bvkhd->bvhqk", query_f, key_f, precision=HIGHEST) * score_scale
    row_peak = jnp.max(scores, axis=-1)
    exponent = jnp.exp(scores - row_peak[..., None])
    exp_total = jnp.sum(exponent, axis=-1)
    partial_sum = jnp.einsum("bvhqk,bvkhd->bvqhd", rounded(exponent), value_f, precision=HIGHEST)
    big_peak = jnp.max(row_peak, axis=1)
    factor = jnp.exp(row_peak - big_peak[:, None])
    big_total = jnp.sum(factor * exp_total, axis=1)
    weighted = jnp.sum(jnp.transpose(factor, (0, 1, 3, 2))[..., None] * partial_sum, axis=1)
    attended = (weighted / jnp.transpose(big_total, (0, 2, 1))[..., None]).astype(jnp.bfloat16)
    delta = jnp.sum(grad_f * attended.astype(jnp.float32), axis=-1)
    probability = jnp.exp(scores - big_peak[:, None, :, :, None]) / big_total[:, None, :, :, None]
    value_grad = jnp.einsum("bvhqk,bqhd->bvkhd", rounded(probability), grad_f, precision=HIGHEST)
    d_prob = jnp.einsum("bqhd,bvkhd->bvhqk", grad_f, value_f, precision=HIGHEST)
    d_score = rounded(probability * (d_prob - jnp.transpose(delta, (0, 2, 1))[:, None, :, :, None]))
    d_query = jnp.einsum("bvhqk,bvkhd->bqhd", d_score, key_f, precision=HIGHEST) * score_scale
    key_grad = jnp.einsum("bvhqk,bqhd->bvkhd", d_score, query_f, precision=HIGHEST) * score_scale
    entry_ids = tile_ids.reshape(-1).astype(jnp.int32)
    entry_count = entry_ids.shape[0]
    positions = jnp.arange(entry_count)
    same_tile = entry_ids[:, None] == entry_ids[None, :]
    earlier = positions[None, :] < positions[:, None]
    first_seen = jnp.logical_not(jnp.any(same_tile & earlier, axis=1))
    same_f = same_tile.astype(jnp.float32)

    def contrib(grads):
        flat_rows = grads.reshape(entry_count, TILE * HD)
        summed = jnp.dot(same_f, flat_rows, precision=HIGHEST)
        kept = jnp.where(first_seen[:, None], rounded(summed), jnp.zeros_like(summed))
        return kept.reshape(entry_count, TILE, HD)

    return (attended.reshape(P_DEV, HD), d_query.astype(jnp.bfloat16).reshape(P_DEV, HD),
            entry_ids, contrib(key_grad), contrib(value_grad))


def reference(queries, key_tiles, value_tiles, visible, destination, d_out):
    query_dev = queries.reshape(N_PTS, P_DEV, HD)
    visible_dev = visible.reshape(N_PTS, QB_DEV, VIS)
    grad_dev = d_out.reshape(N_PTS, P_DEV, HD)

    def per_device(running, pieces):
        keys_acc, values_acc = running
        query_piece, visible_piece, grad_piece = pieces
        attended, d_query, entry_ids, key_part, value_part = device_pass(
            key_tiles, value_tiles, query_piece, visible_piece, grad_piece)
        keys_acc = keys_acc.at[entry_ids].add(key_part)
        values_acc = values_acc.at[entry_ids].add(value_part)
        return (keys_acc, values_acc), (attended, d_query)

    start_acc = (jnp.zeros((KVTILES, TILE, HD), jnp.float32), jnp.zeros((KVTILES, TILE, HD), jnp.float32))
    (keys_acc, values_acc), (attended, d_query) = lax.scan(
        per_device, start_acc, (query_dev, visible_dev, grad_dev))
    attended_rows = attended.reshape(NPTS, HD)
    serial = jnp.zeros((NPTS, HD), jnp.bfloat16).at[destination].set(attended_rows)
    return (serial, d_query.reshape(NPTS, HD), keys_acc.astype(jnp.bfloat16),
            values_acc.astype(jnp.bfloat16))
```

```python
import functools
import math

import jax
import jax.numpy as jnp
from jax import lax
from jax.experimental import pallas as pl
from jax.experimental.pallas import tpu as pltpu
from jax.sharding import PartitionSpec as P

DH = 64
HEADS = 16
DIST = 32


HIGHEST = lax.Precision.HIGHEST


def merged(value, axis, join):
    pieces = jax.tree.map(lambda part: lax.all_gather(part, axis), value)
    head = jax.tree.map(lambda part: part[0], pieces)
    tail = jax.tree.map(lambda part: part[1:], pieces)
    running, _ = lax.scan(lambda running, share: (join(running, share), None), head, tail)
    return running


def pick(table, ids):
    hits = (ids.reshape(-1)[:, None] == jnp.arange(table.shape[0])[None, :]).astype(jnp.bfloat16)
    flat = jnp.dot(
        hits, table.reshape(table.shape[0], -1), preferred_element_type=jnp.float32
    ).astype(table.dtype)
    return flat.reshape(ids.shape + table.shape[1:])


def fetch_tiles(requests, key_tiles, value_tiles):
    asked_ids = lax.all_to_all(requests, "pts", split_axis=0, concat_axis=0, tiled=True)
    safe_ids = jnp.maximum(asked_ids, 0)
    keys_out = pick(key_tiles, safe_ids)
    values_out = pick(value_tiles, safe_ids)
    keys_back = lax.all_to_all(keys_out, "pts", split_axis=0, concat_axis=0, tiled=True)
    values_back = lax.all_to_all(values_out, "pts", split_axis=0, concat_axis=0, tiled=True)
    return (keys_back, values_back, asked_ids)


def refetch_tiles(requests, key_tiles, value_tiles):
    safe_ids = jnp.maximum(
        lax.all_to_all(requests, "pts", split_axis=0, concat_axis=0, tiled=True), 0
    )
    keys_out = pick(key_tiles, safe_ids)
    values_out = pick(value_tiles, safe_ids)
    return (
        lax.all_to_all(keys_out, "pts", split_axis=0, concat_axis=0, tiled=True),
        lax.all_to_all(values_out, "pts", split_axis=0, concat_axis=0, tiled=True),
    )


def widen(stats):
    return jnp.repeat(stats, DH, axis=1)


def local(queries, key_tiles, value_tiles, visible, destination, d_out):
    pts_count = lax.axis_size("pts")
    view_count = lax.axis_size("view")
    kv_dev, tile_keys, local_width = key_tiles.shape
    qb_dev, nvis = visible.shape
    p_dev = queries.shape[0]
    qblock = p_dev // qb_dev
    heads_local = local_width // DH
    group_heads = math.gcd(heads_local, 4)
    group_width = group_heads * DH
    group_total = heads_local // group_heads
    capacity = max(2, min(kv_dev, 2 * DIST // pts_count))
    score_scale = DH ** (-0.5)
    slot_total = pts_count * capacity
    entries = visible.reshape(-1)
    entry_count = entries.shape[0]
    owner_of = entries // kv_dev // view_count
    local_id = entries % kv_dev
    positions = jnp.arange(entry_count)
    same_id = entries[:, None] == entries[None, :]
    earlier = positions[None, :] < positions[:, None]
    first_seen = jnp.logical_not(jnp.any(same_id & earlier, axis=1))
    same_owner = (owner_of[:, None] == owner_of[None, :]) & earlier & first_seen[None, :]
    owner_rank = jnp.sum(same_owner.astype(jnp.int32), axis=1)
    own_slot = owner_of * capacity + owner_rank
    slot_of = jnp.sum(jnp.where(same_id & first_seen[None, :], own_slot[None, :], 0), axis=1)
    slot_grid = jnp.arange(slot_total)
    slot_hit = (own_slot[None, :] == slot_grid[:, None]) & first_seen[None, :]
    requests = (jnp.sum(jnp.where(slot_hit, local_id[None, :] + 1, 0), axis=1) - 1).reshape(
        pts_count, capacity
    )
    slot_table = slot_of.reshape(qb_dev, nvis)

    def block_tiles(fetched):
        flat_tiles = fetched.reshape(slot_total, tile_keys, local_width)
        return pick(flat_tiles, slot_table).reshape(
            qb_dev, nvis * tile_keys, local_width
        )

    fetched_keys, fetched_values, asked = fetch_tiles(requests, key_tiles, value_tiles)
    block_keys = block_tiles(fetched_keys)
    block_values = block_tiles(fetched_values)
    query_blocks = queries.reshape(qb_dev, qblock, local_width)
    key_count = nvis * tile_keys
    peak_list, total_list, weighted_list = ([], [], [])
    for group_number in range(group_total):
        col_start = group_number * group_width
        col_stop = col_start + group_width
        query_part = query_blocks[..., col_start:col_stop].reshape(qb_dev, qblock, group_heads, DH)
        key_part = block_keys[..., col_start:col_stop].reshape(qb_dev, key_count, group_heads, DH)
        value_part = block_values[..., col_start:col_stop].reshape(
            qb_dev, key_count, group_heads, DH
        )
        scores = (
            jnp.einsum("bqhd,bkhd->bhqk", query_part, key_part, preferred_element_type=jnp.float32)
            * score_scale
        )
        local_peak = jnp.max(scores, axis=-1)
        exponent = jnp.exp(scores - local_peak[..., None])
        local_total = jnp.sum(exponent, axis=-1)
        weighted = jnp.einsum(
            "bhqk,bkhd->bqhd",
            exponent.astype(jnp.bfloat16),
            value_part,
            preferred_element_type=jnp.float32,
        )
        peak_list.append(jnp.transpose(local_peak, (0, 2, 1)))
        total_list.append(jnp.transpose(local_total, (0, 2, 1)))
        weighted_list.append(weighted.reshape(qb_dev, qblock, group_width))
    peak_rows = jnp.concatenate(peak_list, axis=-1).reshape(p_dev, heads_local)
    total_rows = jnp.concatenate(total_list, axis=-1).reshape(p_dev, heads_local)
    weighted_rows = jnp.concatenate(weighted_list, axis=-1).reshape(p_dev, local_width)

    def join(first_part, second_part):
        peak_a, total_a, sum_a = first_part
        peak_b, total_b, sum_b = second_part
        peak_top = jnp.maximum(peak_a, peak_b)
        factor_a = jnp.exp(peak_a - peak_top)
        factor_b = jnp.exp(peak_b - peak_top)
        return (
            peak_top,
            factor_a * total_a + factor_b * total_b,
            widen(factor_a) * sum_a + widen(factor_b) * sum_b,
        )

    big_peak, big_total, big_sum = merged((peak_rows, total_rows, weighted_rows), "view", join)
    attended_rows = (big_sum / widen(big_total)).astype(jnp.bfloat16)
    again_keys, again_values = refetch_tiles(requests, key_tiles, value_tiles)
    grad_keys = block_tiles(again_keys)
    grad_values = block_tiles(again_values)
    delta_rows = jnp.sum(
        (d_out.astype(jnp.float32) * attended_rows.astype(jnp.float32)).reshape(
            p_dev, heads_local, DH
        ),
        axis=-1,
    )
    peak_heads = big_peak.reshape(qb_dev, qblock, heads_local)
    total_heads = big_total.reshape(qb_dev, qblock, heads_local)
    delta_heads = delta_rows.reshape(qb_dev, qblock, heads_local)
    grad_blocks = d_out.reshape(qb_dev, qblock, local_width)
    dquery_list, dkey_list, dvalue_list = ([], [], [])
    for group_number in range(group_total):
        col_start = group_number * group_width
        col_stop = col_start + group_width
        head_start = group_number * group_heads
        head_stop = head_start + group_heads
        query_part = query_blocks[..., col_start:col_stop].reshape(qb_dev, qblock, group_heads, DH)
        key_part = grad_keys[..., col_start:col_stop].reshape(qb_dev, key_count, group_heads, DH)
        value_part = grad_values[..., col_start:col_stop].reshape(
            qb_dev, key_count, group_heads, DH
        )
        grad_part = grad_blocks[..., col_start:col_stop].reshape(qb_dev, qblock, group_heads, DH)
        peak_part = jnp.transpose(peak_heads[..., head_start:head_stop], (0, 2, 1))[..., None]
        total_part = jnp.transpose(total_heads[..., head_start:head_stop], (0, 2, 1))[..., None]
        delta_part = jnp.transpose(delta_heads[..., head_start:head_stop], (0, 2, 1))[..., None]
        scores = (
            jnp.einsum("bqhd,bkhd->bhqk", query_part, key_part, preferred_element_type=jnp.float32)
            * score_scale
        )
        probability = jnp.exp(scores - peak_part) / total_part
        value_grad = jnp.einsum(
            "bhqk,bqhd->bkhd",
            probability.astype(jnp.bfloat16),
            grad_part,
            preferred_element_type=jnp.float32,
        )
        d_prob = jnp.einsum(
            "bqhd,bkhd->bhqk", grad_part, value_part, preferred_element_type=jnp.float32
        )
        d_score = (probability * (d_prob - delta_part)).astype(jnp.bfloat16)
        query_grad = (
            jnp.einsum("bhqk,bkhd->bqhd", d_score, key_part, preferred_element_type=jnp.float32)
            * score_scale
        )
        key_grad = (
            jnp.einsum("bhqk,bqhd->bkhd", d_score, query_part, preferred_element_type=jnp.float32)
            * score_scale
        )
        dquery_list.append(query_grad.reshape(qb_dev, qblock, group_width))
        dkey_list.append(key_grad.reshape(qb_dev, key_count, group_width))
        dvalue_list.append(value_grad.reshape(qb_dev, key_count, group_width))
    dquery_local = jnp.concatenate(dquery_list, axis=-1).reshape(p_dev, local_width)
    dkey_blocks = jnp.concatenate(dkey_list, axis=-1)
    dvalue_blocks = jnp.concatenate(dvalue_list, axis=-1)
    d_queries = lax.psum(dquery_local, "view").astype(jnp.bfloat16)
    slot_match = (slot_of[None, :] == slot_grid[:, None]).astype(jnp.float32)

    def per_slot(blocks):
        flat_rows = blocks.reshape(qb_dev * nvis, tile_keys * local_width)
        summed = jnp.dot(
            slot_match, flat_rows, precision=HIGHEST, preferred_element_type=jnp.float32
        )
        return summed.astype(jnp.bfloat16).reshape(pts_count, capacity, tile_keys, local_width)

    back_keys, back_values = (
        lax.all_to_all(per_slot(dkey_blocks), "pts", split_axis=0, concat_axis=0, tiled=True),
        lax.all_to_all(per_slot(dvalue_blocks), "pts", split_axis=0, concat_axis=0, tiled=True),
    )
    owner_match = (asked.reshape(-1)[None, :] == jnp.arange(kv_dev)[:, None]).astype(jnp.bfloat16)
    d_keys = (
        jnp.dot(
            owner_match,
            back_keys.reshape(slot_total, tile_keys * local_width),
            preferred_element_type=jnp.float32,
        )
        .astype(jnp.bfloat16)
        .reshape(kv_dev, tile_keys, local_width)
    )
    d_values = (
        jnp.dot(
            owner_match,
            back_values.reshape(slot_total, tile_keys * local_width),
            preferred_element_type=jnp.float32,
        )
        .astype(jnp.bfloat16)
        .reshape(kv_dev, tile_keys, local_width)
    )
    per_peer = p_dev // pts_count
    target = destination // p_dev
    row_place = destination % p_dev
    peer_hits = (target[:, None] == jnp.arange(pts_count)[None, :]).astype(jnp.int32)
    ahead = jnp.arange(p_dev)[None, :] < jnp.arange(p_dev)[:, None]
    before = jnp.dot(
        ahead.astype(jnp.bfloat16),
        peer_hits.astype(jnp.bfloat16),
        preferred_element_type=jnp.float32,
    ).astype(jnp.int32)
    send_rank = jnp.sum(before * peer_hits, axis=1)
    send_position = target * per_peer + send_rank
    row_numbers = jnp.arange(p_dev, dtype=jnp.int32)
    send_inverse = jnp.zeros((p_dev,), jnp.int32).at[send_position].set(row_numbers)
    rows_out = attended_rows[send_inverse].reshape(pts_count, per_peer, local_width)
    places_out = row_place[send_inverse].reshape(pts_count, per_peer)
    got_rows, got_places = (
        lax.all_to_all(rows_out, "pts", split_axis=0, concat_axis=0, tiled=True),
        lax.all_to_all(places_out, "pts", split_axis=0, concat_axis=0, tiled=True),
    )
    place_inverse = jnp.zeros((p_dev,), jnp.int32).at[got_places.reshape(-1)].set(row_numbers)
    attended = got_rows.reshape(p_dev, local_width)[place_inverse]
    return (attended, d_queries, d_keys, d_values)


MESH = pl.DeviceIdType.MESH
WIDE = 2 * DH
TILE = 16
HIDDEN = -1e30
META_ROWS = 8


def remote(src, dst, send_sem, recv_sem, place):
    return pltpu.make_async_remote_copy(
        src_ref=src,
        dst_ref=dst,
        send_sem=send_sem,
        recv_sem=recv_sem,
        device_id=place,
        device_id_type=MESH,
    )


def head_kernel(
    pts,
    view,
    q_ref,
    k_ref,
    v_ref,
    vis_ref,
    dest_ref,
    g_ref,
    att_ref,
    dq_ref,
    dk_ref,
    dv_ref,
    meta,
    kv_out,
    kv,
    qd_out,
    qd,
    bias,
    place,
    rows,
    grads,
    od_out,
    od,
    dkv_out,
    dkv,
    meta_s,
    meta_r,
    kv_s,
    kv_r,
    qd_s,
    qd_r,
    od_s,
    od_r,
    dkv_s,
    dkv_r,
):
    z = lax.axis_index("pts")
    w = lax.axis_index("view")
    peers = pts * view
    me = z * view + w
    p_dev = q_ref.shape[0]
    qb_dev, nvis = vis_ref.shape
    qblock = p_dev // qb_dev
    held = k_ref.shape[0]
    keys = peers * held
    dest_rows = dest_ref.shape[0]

    barrier = pltpu.get_barrier_semaphore()
    others = []
    for step in range(1, peers):
        other = lax.rem(me + step, peers)
        others.append((other, other // view, lax.rem(other, view)))
    column = []
    for step in range(1, pts):
        column.append(lax.rem(z + step, pts))
    for _, oz, ow in others:
        pl.semaphore_signal(barrier, inc=1, device_id={"pts": oz, "view": ow}, device_id_type=MESH)

    meta[me] = jnp.zeros((META_ROWS, WIDE), jnp.int32)
    meta[me, 0:qb_dev, 0:nvis] = vis_ref[...]
    meta[me, qb_dev : qb_dev + dest_rows, :] = dest_ref[...]
    for pair in range(peers // 2):
        cols = slice(pair * WIDE, (pair + 1) * WIDE)
        kt, vt = k_ref[:, cols], v_ref[:, cols]
        kv_out[2 * pair] = jnp.concatenate([kt[:, :DH], vt[:, :DH]], axis=1)
        kv_out[2 * pair + 1] = jnp.concatenate([kt[:, DH:], vt[:, DH:]], axis=1)
    pl.semaphore_wait(barrier, peers - 1)

    sends = []

    def start(copy):
        copy.start()
        sends.append(copy)

    for other, oz, ow in others:
        spot = {"pts": oz, "view": ow}
        start(remote(meta.at[me], meta.at[me], meta_s.at[other], meta_r.at[me], spot))
    for other, oz, ow in others:
        spot = {"pts": oz, "view": ow}
        start(remote(kv_out.at[other], kv.at[me], kv_s.at[other], kv_r.at[me], spot))
    kv[me] = kv_out[me]

    for peer in range(pts):
        parts = []
        for half in range(view):
            at = (peer * view + half) * DH
            tile = (at // WIDE) * WIDE
            off = at - tile
            parts.append((q_ref[:, tile + off : tile + off + DH], g_ref[:, tile + off : tile + off + DH]))
        qh, gh = parts[0]
        packed = jnp.concatenate([qh, gh], axis=1)
        for half in range(1, view):
            qn, gn = parts[half]
            packed = jnp.where(w == half, jnp.concatenate([qn, gn], axis=1), packed)
        qd_out[peer] = packed
    for oz in column:
        spot = {"pts": oz, "view": w}
        start(remote(qd_out.at[oz], qd.at[z], qd_s.at[oz], qd_r.at[z], spot))
    qd[z] = qd_out[z]

    for other, oz, ow in others:
        remote(meta.at[me], meta.at[other], meta_s.at[other], meta_r.at[other], {"pts": oz, "view": ow}).wait_recv()

    tile_of = lax.broadcasted_iota(jnp.int32, (META_ROWS, keys), 1) // (keys // (peers * (held // TILE)))
    for p in range(pts):
        hit = None
        for half in range(view):
            ids = meta[p * view + half]
            for i in range(nvis):
                one = ids[:, i : i + 1] == tile_of
                hit = one if hit is None else hit | one
        bias[p] = jnp.where(hit, 0.0, HIDDEN)
    row_number = lax.broadcasted_iota(jnp.int32, (pts * p_dev, WIDE), 0)
    for p in range(pts):
        for c in range(dest_rows):
            line = meta[p * view, qb_dev + c : qb_dev + c + 1, :]
            at = p * p_dev + c * WIDE
            place[:, at : at + WIDE] = jnp.where(row_number == line, 1.0, 0.0).astype(jnp.bfloat16)

    for other, oz, ow in others:
        remote(kv_out.at[0], kv.at[other], kv_s.at[other], kv_r.at[other], {"pts": oz, "view": ow}).wait_recv()
    grads[...] = jnp.zeros_like(grads)

    lower = lax.broadcasted_iota(jnp.int32, (qblock, WIDE), 1) < DH
    zero = jnp.zeros((), jnp.bfloat16)
    scale = DH**-0.5
    nt = (((1,), (1,)), ((), ()))

    def block(p, b):
        both = kv[...].reshape(keys, WIDE)
        mixed = qd[p, b * qblock : (b + 1) * qblock, :]
        query = jnp.where(lower, mixed * jnp.asarray(scale, jnp.bfloat16), zero)
        grad = jnp.where(lower, zero, mixed)
        scores = lax.dot_general(query, both, nt, preferred_element_type=jnp.float32)
        scores = scores + bias[p, b : b + 1, :]
        d_prob = lax.dot_general(grad, both, nt, preferred_element_type=jnp.float32)
        peak = jnp.max(scores, axis=1, keepdims=True)
        weight = jnp.exp(scores - peak)
        total = jnp.sum(weight, axis=1, keepdims=True)
        inverse = 1.0 / total
        summed = jnp.dot(weight.astype(jnp.bfloat16), both, preferred_element_type=jnp.float32)
        out = (summed / total).astype(jnp.bfloat16)
        delta = jnp.sum(
            grad.astype(jnp.float32) * out.astype(jnp.float32), axis=1, keepdims=True
        )
        prob = weight * inverse
        d_score = (prob * (d_prob - delta)).astype(jnp.bfloat16)
        d_query = jnp.dot(d_score, both, preferred_element_type=jnp.float32) * scale
        left = jnp.concatenate([query, grad], axis=0)
        right = jnp.concatenate([d_score, prob.astype(jnp.bfloat16)], axis=0)
        grads[...] += jnp.dot(left.T, right, preferred_element_type=jnp.float32)
        return jnp.where(lower, d_query.astype(jnp.bfloat16), out)

    def step_body(step, carry):
        p = lax.rem(z + step, pts)

        @pl.when(step > 0)
        def _():
            remote(qd_out.at[0], qd.at[p], qd_s.at[p], qd_r.at[p], {"pts": p, "view": w}).wait_recv()

        for b in range(qb_dev):
            rows[p, b * qblock : (b + 1) * qblock, :] = block(p, b)
        return carry

    lax.fori_loop(0, pts, step_body, 0)

    dkv_out[...] = grads[...].T.astype(jnp.bfloat16).reshape(dkv_out.shape)
    for other, oz, ow in others:
        spot = {"pts": oz, "view": ow}
        start(remote(dkv_out.at[other], dkv.at[me], dkv_s.at[other], dkv_r.at[me], spot))
    dkv[me] = dkv_out[me]

    every = rows[...].reshape(pts * p_dev, WIDE)
    moved = jnp.dot(place[...], every, preferred_element_type=jnp.float32).astype(jnp.bfloat16)
    lower_all = lax.broadcasted_iota(jnp.int32, (pts * p_dev, WIDE), 1) < DH
    od_out[...] = jnp.where(lower_all, every, moved).reshape(od_out.shape)
    for other, oz, ow in others:
        spot = {"pts": oz, "view": ow}
        start(remote(od_out.at[oz], od.at[me], od_s.at[other], od_r.at[me], spot))
    od[me] = od_out[z]

    for other, oz, ow in others:
        remote(dkv_out.at[0], dkv.at[other], dkv_s.at[other], dkv_r.at[other], {"pts": oz, "view": ow}).wait_recv()
    for pair in range(peers // 2):
        cols = slice(pair * WIDE, (pair + 1) * WIDE)
        even, odd = dkv[2 * pair], dkv[2 * pair + 1]
        dk_ref[:, cols] = jnp.concatenate([even[:, :DH], odd[:, :DH]], axis=1)
        dv_ref[:, cols] = jnp.concatenate([even[:, DH:], odd[:, DH:]], axis=1)
    for other, oz, ow in others:
        remote(od_out.at[0], od.at[other], od_s.at[other], od_r.at[other], {"pts": oz, "view": ow}).wait_recv()
    for pair in range(peers // 2):
        cols = slice(pair * WIDE, (pair + 1) * WIDE)
        even, odd = od[2 * pair], od[2 * pair + 1]
        dq_ref[:, cols] = jnp.concatenate([even[:, :DH], odd[:, :DH]], axis=1)
        att_ref[:, cols] = jnp.concatenate([even[:, DH:], odd[:, DH:]], axis=1)
    for copy in sends:
        copy.wait_send()


def by_head(queries, key_tiles, value_tiles, visible, destination, d_out):
    pts = lax.axis_size("pts")
    view = lax.axis_size("view")
    peers = pts * view
    kv_dev, tile_keys, width = key_tiles.shape
    held = kv_dev * tile_keys
    p_dev = queries.shape[0]
    keys = peers * held
    whole = pl.BlockSpec(memory_space=pltpu.VMEM)
    bf = jnp.bfloat16
    dma = pltpu.SemaphoreType.DMA
    att, dq, dk, dv = pl.pallas_call(
        functools.partial(head_kernel, pts, view),
        out_shape=(
            jax.ShapeDtypeStruct((p_dev, width), bf),
            jax.ShapeDtypeStruct((p_dev, width), bf),
            jax.ShapeDtypeStruct((held, width), bf),
            jax.ShapeDtypeStruct((held, width), bf),
        ),
        in_specs=[whole] * 6,
        out_specs=(whole,) * 4,
        scratch_shapes=[
            pltpu.VMEM((peers, META_ROWS, WIDE), jnp.int32),
            pltpu.VMEM((peers, held, WIDE), bf),
            pltpu.VMEM((peers, held, WIDE), bf),
            pltpu.VMEM((pts, p_dev, WIDE), bf),
            pltpu.VMEM((pts, p_dev, WIDE), bf),
            pltpu.VMEM((pts, META_ROWS, keys), jnp.float32),
            pltpu.VMEM((pts * p_dev, pts * p_dev), bf),
            pltpu.VMEM((pts, p_dev, WIDE), bf),
            pltpu.VMEM((WIDE, keys), jnp.float32),
            pltpu.VMEM((pts, p_dev, WIDE), bf),
            pltpu.VMEM((peers, p_dev, WIDE), bf),
            pltpu.VMEM((peers, held, WIDE), bf),
            pltpu.VMEM((peers, held, WIDE), bf),
            dma((peers,)),
            dma((peers,)),
            dma((peers,)),
            dma((peers,)),
            dma((pts,)),
            dma((pts,)),
            dma((peers,)),
            dma((peers,)),
            dma((peers,)),
            dma((peers,)),
        ],
        compiler_params=pltpu.CompilerParams(
            collective_id=0, has_side_effects=True, vmem_limit_bytes=48 * 1024 * 1024
        ),
        cost_estimate=pl.CostEstimate(
            flops=14 * pts * p_dev * keys * DH,
            bytes_accessed=6 * p_dev * width * 2,
            transcendentals=pts * p_dev * keys,
        ),
    )(
        queries,
        key_tiles.reshape(held, width),
        value_tiles.reshape(held, width),
        visible,
        destination.reshape(p_dev // WIDE, WIDE),
        d_out,
    )
    return (att, dq, dk.reshape(key_tiles.shape), dv.reshape(value_tiles.shape))


def solution(mesh):
    in_specs = (
        P(("scene", "pts"), "head"),
        P(("scene", "pts", "view"), None, "head"),
        P(("scene", "pts", "view"), None, "head"),
        P(("scene", "pts"), "view"),
        P(("scene", "pts")),
        P(("scene", "pts"), "head"),
    )
    out_specs = (
        P(("scene", "pts"), "head"),
        P(("scene", "pts"), "head"),
        P(("scene", "pts", "view"), None, "head"),
        P(("scene", "pts", "view"), None, "head"),
    )
    heads_local = HEADS // mesh.shape["head"]
    per_device = local
    if heads_local == mesh.shape["pts"] * mesh.shape["view"] and heads_local % 2 == 0:
        per_device = by_head
    return jax.shard_map(per_device, mesh=mesh, in_specs=in_specs, out_specs=out_specs, check_vma=False)
```

```python
import functools
import math

import jax
import jax.numpy as jnp
from jax import lax
from jax.experimental import pallas as pl
from jax.experimental.pallas import tpu as pltpu
from jax.sharding import PartitionSpec as P

DH = 64
HEADS = 16
DIST = 32


HIGHEST = lax.Precision.HIGHEST


def merged(value, axis, join):
    pieces = jax.tree.map(lambda part: lax.all_gather(part, axis), value)
    head = jax.tree.map(lambda part: part[0], pieces)
    tail = jax.tree.map(lambda part: part[1:], pieces)
    running, _ = lax.scan(lambda running, share: (join(running, share), None), head, tail)
    return running


def pick(table, ids):
    hits = (ids.reshape(-1)[:, None] == jnp.arange(table.shape[0])[None, :]).astype(jnp.bfloat16)
    flat = jnp.dot(
        hits, table.reshape(table.shape[0], -1), preferred_element_type=jnp.float32
    ).astype(table.dtype)
    return flat.reshape(ids.shape + table.shape[1:])


def fetch_tiles(requests, key_tiles, value_tiles):
    asked_ids = lax.all_to_all(requests, "pts", split_axis=0, concat_axis=0, tiled=True)
    safe_ids = jnp.maximum(asked_ids, 0)
    keys_out = pick(key_tiles, safe_ids)
    values_out = pick(value_tiles, safe_ids)
    keys_back = lax.all_to_all(keys_out, "pts", split_axis=0, concat_axis=0, tiled=True)
    values_back = lax.all_to_all(values_out, "pts", split_axis=0, concat_axis=0, tiled=True)
    return (keys_back, values_back, asked_ids)


def refetch_tiles(requests, key_tiles, value_tiles):
    safe_ids = jnp.maximum(
        lax.all_to_all(requests, "pts", split_axis=0, concat_axis=0, tiled=True), 0
    )
    keys_out = pick(key_tiles, safe_ids)
    values_out = pick(value_tiles, safe_ids)
    return (
        lax.all_to_all(keys_out, "pts", split_axis=0, concat_axis=0, tiled=True),
        lax.all_to_all(values_out, "pts", split_axis=0, concat_axis=0, tiled=True),
    )


def widen(stats):
    return jnp.repeat(stats, DH, axis=1)


def local(queries, key_tiles, value_tiles, visible, destination, d_out):
    pts_count = lax.axis_size("pts")
    view_count = lax.axis_size("view")
    kv_dev, tile_keys, local_width = key_tiles.shape
    qb_dev, nvis = visible.shape
    p_dev = queries.shape[0]
    qblock = p_dev // qb_dev
    heads_local = local_width // DH
    group_heads = math.gcd(heads_local, 4)
    group_width = group_heads * DH
    group_total = heads_local // group_heads
    capacity = max(2, min(kv_dev, 2 * DIST // pts_count))
    score_scale = DH ** (-0.5)
    slot_total = pts_count * capacity
    entries = visible.reshape(-1)
    entry_count = entries.shape[0]
    owner_of = entries // kv_dev // view_count
    local_id = entries % kv_dev
    positions = jnp.arange(entry_count)
    same_id = entries[:, None] == entries[None, :]
    earlier = positions[None, :] < positions[:, None]
    first_seen = jnp.logical_not(jnp.any(same_id & earlier, axis=1))
    same_owner = (owner_of[:, None] == owner_of[None, :]) & earlier & first_seen[None, :]
    owner_rank = jnp.sum(same_owner.astype(jnp.int32), axis=1)
    own_slot = owner_of * capacity + owner_rank
    slot_of = jnp.sum(jnp.where(same_id & first_seen[None, :], own_slot[None, :], 0), axis=1)
    slot_grid = jnp.arange(slot_total)
    slot_hit = (own_slot[None, :] == slot_grid[:, None]) & first_seen[None, :]
    requests = (jnp.sum(jnp.where(slot_hit, local_id[None, :] + 1, 0), axis=1) - 1).reshape(
        pts_count, capacity
    )
    slot_table = slot_of.reshape(qb_dev, nvis)

    def block_tiles(fetched):
        flat_tiles = fetched.reshape(slot_total, tile_keys, local_width)
        return pick(flat_tiles, slot_table).reshape(
            qb_dev, nvis * tile_keys, local_width
        )

    fetched_keys, fetched_values, asked = fetch_tiles(requests, key_tiles, value_tiles)
    block_keys = block_tiles(fetched_keys)
    block_values = block_tiles(fetched_values)
    query_blocks = queries.reshape(qb_dev, qblock, local_width)
    key_count = nvis * tile_keys
    peak_list, total_list, weighted_list = ([], [], [])
    for group_number in range(group_total):
        col_start = group_number * group_width
        col_stop = col_start + group_width
        query_part = query_blocks[..., col_start:col_stop].reshape(qb_dev, qblock, group_heads, DH)
        key_part = block_keys[..., col_start:col_stop].reshape(qb_dev, key_count, group_heads, DH)
        value_part = block_values[..., col_start:col_stop].reshape(
            qb_dev, key_count, group_heads, DH
        )
        scores = (
            jnp.einsum("bqhd,bkhd->bhqk", query_part, key_part, preferred_element_type=jnp.float32)
            * score_scale
        )
        local_peak = jnp.max(scores, axis=-1)
        exponent = jnp.exp(scores - local_peak[..., None])
        local_total = jnp.sum(exponent, axis=-1)
        weighted = jnp.einsum(
            "bhqk,bkhd->bqhd",
            exponent.astype(jnp.bfloat16),
            value_part,
            preferred_element_type=jnp.float32,
        )
        peak_list.append(jnp.transpose(local_peak, (0, 2, 1)))
        total_list.append(jnp.transpose(local_total, (0, 2, 1)))
        weighted_list.append(weighted.reshape(qb_dev, qblock, group_width))
    peak_rows = jnp.concatenate(peak_list, axis=-1).reshape(p_dev, heads_local)
    total_rows = jnp.concatenate(total_list, axis=-1).reshape(p_dev, heads_local)
    weighted_rows = jnp.concatenate(weighted_list, axis=-1).reshape(p_dev, local_width)

    def join(first_part, second_part):
        peak_a, total_a, sum_a = first_part
        peak_b, total_b, sum_b = second_part
        peak_top = jnp.maximum(peak_a, peak_b)
        factor_a = jnp.exp(peak_a - peak_top)
        factor_b = jnp.exp(peak_b - peak_top)
        return (
            peak_top,
            factor_a * total_a + factor_b * total_b,
            widen(factor_a) * sum_a + widen(factor_b) * sum_b,
        )

    big_peak, big_total, big_sum = merged((peak_rows, total_rows, weighted_rows), "view", join)
    attended_rows = (big_sum / widen(big_total)).astype(jnp.bfloat16)
    again_keys, again_values = refetch_tiles(requests, key_tiles, value_tiles)
    grad_keys = block_tiles(again_keys)
    grad_values = block_tiles(again_values)
    delta_rows = jnp.sum(
        (d_out.astype(jnp.float32) * attended_rows.astype(jnp.float32)).reshape(
            p_dev, heads_local, DH
        ),
        axis=-1,
    )
    peak_heads = big_peak.reshape(qb_dev, qblock, heads_local)
    total_heads = big_total.reshape(qb_dev, qblock, heads_local)
    delta_heads = delta_rows.reshape(qb_dev, qblock, heads_local)
    grad_blocks = d_out.reshape(qb_dev, qblock, local_width)
    dquery_list, dkey_list, dvalue_list = ([], [], [])
    for group_number in range(group_total):
        col_start = group_number * group_width
        col_stop = col_start + group_width
        head_start = group_number * group_heads
        head_stop = head_start + group_heads
        query_part = query_blocks[..., col_start:col_stop].reshape(qb_dev, qblock, group_heads, DH)
        key_part = grad_keys[..., col_start:col_stop].reshape(qb_dev, key_count, group_heads, DH)
        value_part = grad_values[..., col_start:col_stop].reshape(
            qb_dev, key_count, group_heads, DH
        )
        grad_part = grad_blocks[..., col_start:col_stop].reshape(qb_dev, qblock, group_heads, DH)
        peak_part = jnp.transpose(peak_heads[..., head_start:head_stop], (0, 2, 1))[..., None]
        total_part = jnp.transpose(total_heads[..., head_start:head_stop], (0, 2, 1))[..., None]
        delta_part = jnp.transpose(delta_heads[..., head_start:head_stop], (0, 2, 1))[..., None]
        scores = (
            jnp.einsum("bqhd,bkhd->bhqk", query_part, key_part, preferred_element_type=jnp.float32)
            * score_scale
        )
        probability = jnp.exp(scores - peak_part) / total_part
        value_grad = jnp.einsum(
            "bhqk,bqhd->bkhd",
            probability.astype(jnp.bfloat16),
            grad_part,
            preferred_element_type=jnp.float32,
        )
        d_prob = jnp.einsum(
            "bqhd,bkhd->bhqk", grad_part, value_part, preferred_element_type=jnp.float32
        )
        d_score = (probability * (d_prob - delta_part)).astype(jnp.bfloat16)
        query_grad = (
            jnp.einsum("bhqk,bkhd->bqhd", d_score, key_part, preferred_element_type=jnp.float32)
            * score_scale
        )
        key_grad = (
            jnp.einsum("bhqk,bqhd->bkhd", d_score, query_part, preferred_element_type=jnp.float32)
            * score_scale
        )
        dquery_list.append(query_grad.reshape(qb_dev, qblock, group_width))
        dkey_list.append(key_grad.reshape(qb_dev, key_count, group_width))
        dvalue_list.append(value_grad.reshape(qb_dev, key_count, group_width))
    dquery_local = jnp.concatenate(dquery_list, axis=-1).reshape(p_dev, local_width)
    dkey_blocks = jnp.concatenate(dkey_list, axis=-1)
    dvalue_blocks = jnp.concatenate(dvalue_list, axis=-1)
    d_queries = lax.psum(dquery_local, "view").astype(jnp.bfloat16)
    slot_match = (slot_of[None, :] == slot_grid[:, None]).astype(jnp.float32)

    def per_slot(blocks):
        flat_rows = blocks.reshape(qb_dev * nvis, tile_keys * local_width)
        summed = jnp.dot(
            slot_match, flat_rows, precision=HIGHEST, preferred_element_type=jnp.float32
        )
        return summed.astype(jnp.bfloat16).reshape(pts_count, capacity, tile_keys, local_width)

    back_keys, back_values = (
        lax.all_to_all(per_slot(dkey_blocks), "pts", split_axis=0, concat_axis=0, tiled=True),
        lax.all_to_all(per_slot(dvalue_blocks), "pts", split_axis=0, concat_axis=0, tiled=True),
    )
    owner_match = (asked.reshape(-1)[None, :] == jnp.arange(kv_dev)[:, None]).astype(jnp.bfloat16)
    d_keys = (
        jnp.dot(
            owner_match,
            back_keys.reshape(slot_total, tile_keys * local_width),
            preferred_element_type=jnp.float32,
        )
        .astype(jnp.bfloat16)
        .reshape(kv_dev, tile_keys, local_width)
    )
    d_values = (
        jnp.dot(
            owner_match,
            back_values.reshape(slot_total, tile_keys * local_width),
            preferred_element_type=jnp.float32,
        )
        .astype(jnp.bfloat16)
        .reshape(kv_dev, tile_keys, local_width)
    )
    per_peer = p_dev // pts_count
    target = destination // p_dev
    row_place = destination % p_dev
    peer_hits = (target[:, None] == jnp.arange(pts_count)[None, :]).astype(jnp.int32)
    ahead = jnp.arange(p_dev)[None, :] < jnp.arange(p_dev)[:, None]
    before = jnp.dot(
        ahead.astype(jnp.bfloat16),
        peer_hits.astype(jnp.bfloat16),
        preferred_element_type=jnp.float32,
    ).astype(jnp.int32)
    send_rank = jnp.sum(before * peer_hits, axis=1)
    send_position = target * per_peer + send_rank
    row_numbers = jnp.arange(p_dev, dtype=jnp.int32)
    send_inverse = jnp.zeros((p_dev,), jnp.int32).at[send_position].set(row_numbers)
    rows_out = attended_rows[send_inverse].reshape(pts_count, per_peer, local_width)
    places_out = row_place[send_inverse].reshape(pts_count, per_peer)
    got_rows, got_places = (
        lax.all_to_all(rows_out, "pts", split_axis=0, concat_axis=0, tiled=True),
        lax.all_to_all(places_out, "pts", split_axis=0, concat_axis=0, tiled=True),
    )
    place_inverse = jnp.zeros((p_dev,), jnp.int32).at[got_places.reshape(-1)].set(row_numbers)
    attended = got_rows.reshape(p_dev, local_width)[place_inverse]
    return (attended, d_queries, d_keys, d_values)


MESH = pl.DeviceIdType.MESH
WIDE = 2 * DH
TILE = 16
HIDDEN = -1e30
ROOM = 63 * 1024 * 1024
META_ROWS = 8


def remote(src, dst, send_sem, recv_sem, place):
    return pltpu.make_async_remote_copy(
        src_ref=src,
        dst_ref=dst,
        send_sem=send_sem,
        recv_sem=recv_sem,
        device_id=place,
        device_id_type=MESH,
    )


def head_kernel(
    pts,
    view,
    q_hbm,
    k_hbm,
    v_hbm,
    vis_hbm,
    dest_hbm,
    g_hbm,
    att,
    dq,
    dkv,
    q_ref,
    k_ref,
    v_ref,
    vis_ref,
    dest_ref,
    g_ref,
    meta,
    kv_out,
    kv,
    qd_out,
    qd,
    bias,
    place,
    rows,
    grads,
    att_out,
    dq_out,
    dkv_out,
    load_s,
    meta_s,
    meta_r,
    kv_s,
    kv_r,
    qd_s,
    qd_r,
    att_s,
    att_r,
    dq_s,
    dq_r,
    dkv_s,
    dkv_r,
):
    z = lax.axis_index("pts")
    w = lax.axis_index("view")
    peers = pts * view
    me = z * view + w
    p_dev = q_ref.shape[0]
    qb_dev, nvis = vis_ref.shape
    qblock = p_dev // qb_dev
    held = k_ref.shape[0]
    keys = peers * held
    dest_rows = dest_ref.shape[0]

    barrier = pltpu.get_barrier_semaphore()
    others = []
    for step in range(1, peers):
        other = lax.rem(me + step, peers)
        others.append((other, other // view, lax.rem(other, view)))
    column = []
    for step in range(1, pts):
        column.append(lax.rem(z + step, pts))
    for _, oz, ow in others:
        pl.semaphore_signal(barrier, inc=1, device_id={"pts": oz, "view": ow}, device_id_type=MESH)

    loads = []
    pairs = (
        (k_hbm, k_ref),
        (v_hbm, v_ref),
        (vis_hbm, vis_ref),
        (dest_hbm, dest_ref),
        (q_hbm, q_ref),
        (g_hbm, g_ref),
    )
    for number, (source, target) in enumerate(pairs):
        load = pltpu.make_async_copy(source, target, load_s.at[number])
        load.start()
        loads.append(load)
    meta[me] = jnp.zeros((META_ROWS, WIDE), jnp.int32)
    for load in loads[:4]:
        load.wait()
    meta[me, 0:qb_dev, 0:nvis] = vis_ref[...]
    meta[me, qb_dev : qb_dev + dest_rows, :] = dest_ref[...]
    for pair in range(peers // 2):
        cols = slice(pair * WIDE, (pair + 1) * WIDE)
        kt, vt = k_ref[:, cols], v_ref[:, cols]
        kv_out[2 * pair] = jnp.concatenate([kt[:, :DH], vt[:, :DH]], axis=1)
        kv_out[2 * pair + 1] = jnp.concatenate([kt[:, DH:], vt[:, DH:]], axis=1)
    pl.semaphore_wait(barrier, peers - 1)

    sends = []

    def start(copy):
        copy.start()
        sends.append(copy)

    for other, oz, ow in others:
        spot = {"pts": oz, "view": ow}
        start(remote(meta.at[me], meta.at[me], meta_s.at[other], meta_r.at[me], spot))
    for other, oz, ow in others:
        spot = {"pts": oz, "view": ow}
        start(remote(kv_out.at[other], kv.at[me], kv_s.at[other], kv_r.at[me], spot))
    kv[me] = kv_out[me]
    for load in loads[4:]:
        load.wait()

    for peer in range(pts):
        parts = []
        for half in range(view):
            at = (peer * view + half) * DH
            tile = (at // WIDE) * WIDE
            off = at - tile
            parts.append((q_ref[:, tile + off : tile + off + DH], g_ref[:, tile + off : tile + off + DH]))
        qh, gh = parts[0]
        packed = jnp.concatenate([qh, gh], axis=1)
        for half in range(1, view):
            qn, gn = parts[half]
            packed = jnp.where(w == half, jnp.concatenate([qn, gn], axis=1), packed)
        qd_out[peer] = packed
    for oz in column:
        spot = {"pts": oz, "view": w}
        start(remote(qd_out.at[oz], qd.at[z], qd_s.at[oz], qd_r.at[z], spot))
    qd[z] = qd_out[z]

    for other, oz, ow in others:
        remote(meta.at[me], meta.at[other], meta_s.at[other], meta_r.at[other], {"pts": oz, "view": ow}).wait_recv()

    tile_of = lax.broadcasted_iota(jnp.int32, (META_ROWS, keys), 1) // (keys // (peers * (held // TILE)))
    for p in range(pts):
        hit = None
        for half in range(view):
            ids = meta[p * view + half]
            for i in range(nvis):
                one = ids[:, i : i + 1] == tile_of
                hit = one if hit is None else hit | one
        bias[p] = jnp.where(hit, 0.0, HIDDEN)
    row_number = lax.broadcasted_iota(jnp.int32, (pts * p_dev, WIDE), 0)
    for p in range(pts):
        for c in range(dest_rows):
            line = meta[p * view, qb_dev + c : qb_dev + c + 1, :]
            at = p * p_dev + c * WIDE
            place[:, at : at + WIDE] = jnp.where(row_number == line, 1.0, 0.0).astype(jnp.bfloat16)

    for other, oz, ow in others:
        remote(kv_out.at[0], kv.at[other], kv_s.at[other], kv_r.at[other], {"pts": oz, "view": ow}).wait_recv()
    grads[...] = jnp.zeros_like(grads)

    lower = lax.broadcasted_iota(jnp.int32, (qblock, WIDE), 1) < DH
    zero = jnp.zeros((), jnp.bfloat16)
    scale = DH**-0.5
    nt = (((1,), (1,)), ((), ()))

    def block(p, b):
        both = kv[...].reshape(keys, WIDE)
        mixed = qd[p, b * qblock : (b + 1) * qblock, :]
        query = jnp.where(lower, mixed * jnp.asarray(scale, jnp.bfloat16), zero)
        grad = jnp.where(lower, zero, mixed)
        scores = lax.dot_general(query, both, nt, preferred_element_type=jnp.float32)
        scores = scores + bias[p, b : b + 1, :]
        d_prob = lax.dot_general(grad, both, nt, preferred_element_type=jnp.float32)
        peak = jnp.max(scores, axis=1, keepdims=True)
        weight = jnp.exp(scores - peak)
        total = jnp.sum(weight, axis=1, keepdims=True)
        inverse = 1.0 / total
        summed = jnp.dot(weight.astype(jnp.bfloat16), both, preferred_element_type=jnp.float32)
        out = (summed / total).astype(jnp.bfloat16)
        delta = jnp.sum(
            grad.astype(jnp.float32) * out.astype(jnp.float32), axis=1, keepdims=True
        )
        prob = weight * inverse
        d_score = (prob * (d_prob - delta)).astype(jnp.bfloat16)
        d_query = jnp.dot(d_score, both, preferred_element_type=jnp.float32) * scale
        left = jnp.concatenate([query, grad], axis=0)
        right = jnp.concatenate([d_score, prob.astype(jnp.bfloat16)], axis=0)
        grads[...] += jnp.dot(left.T, right, preferred_element_type=jnp.float32)
        return jnp.where(lower, d_query.astype(jnp.bfloat16), out)

    half_rows = p_dev // 2
    twin = {"pts": z, "view": lax.rem(w + 1, view)}

    def fold(upper, lower_half, side):
        at = slice(side * DH, (side + 1) * DH)
        return jnp.concatenate([upper[:, at], lower_half[:, at]], axis=1)

    def dq_copy(p):
        spot = {"pts": p, "view": w}
        return remote(dq_out.at[p], dq.at[me], dq_s.at[p], dq_r.at[me], spot)

    def twin_copy(source, target, sent, got, number):
        return remote(source, target.at[number], sent, got.at[number], twin)

    def step_body(step, carry):
        p = lax.rem(z + step, pts)

        @pl.when(step > 0)
        def _():
            remote(qd_out.at[0], qd.at[p], qd_s.at[p], qd_r.at[p], {"pts": p, "view": w}).wait_recv()

        for b in range(qb_dev):
            rows[p, b * qblock : (b + 1) * qblock, :] = block(p, b)
        dq_out[p] = fold(rows[p, :half_rows, :], rows[p, half_rows:, :], 0)

        @pl.when(step > 0)
        def _():
            dq_copy(p).start()

        return carry

    lax.fori_loop(0, pts, step_body, 0)
    kept = []
    start(twin_copy(dq_out.at[z], dq, dq_s.at[z], dq_r, me))
    dq_own = pltpu.make_async_copy(dq_out.at[z], dq.at[me], load_s.at[0])
    dq_own.start()
    kept.append(dq_own)

    def send_att():
        every = rows[...].reshape(pts * p_dev, WIDE)
        moved = jnp.dot(place[...], every, preferred_element_type=jnp.float32)
        for p in range(pts):
            top = moved[p * p_dev : p * p_dev + half_rows]
            low = moved[p * p_dev + half_rows : (p + 1) * p_dev]
            att_out[p] = fold(top, low, 1).astype(jnp.bfloat16)
        for oz in column:
            spot = {"pts": oz, "view": w}
            start(remote(att_out.at[oz], att.at[me], att_s.at[oz], att_r.at[me], spot))
        start(twin_copy(att_out.at[z], att, att_s.at[z], att_r, me))
        att_own = pltpu.make_async_copy(att_out.at[z], att.at[me], load_s.at[1])
        att_own.start()
        kept.append(att_own)

    def send_dkv():
        dkv_out[...] = grads[...].T.astype(jnp.bfloat16).reshape(dkv_out.shape)
        for other, oz, ow in others:
            spot = {"pts": oz, "view": ow}
            start(remote(dkv_out.at[other], dkv.at[me], dkv_s.at[other], dkv_r.at[me], spot))
        dkv_own = pltpu.make_async_copy(dkv_out.at[me], dkv.at[me], load_s.at[2])
        dkv_own.start()
        kept.append(dkv_own)

    send_att()
    send_dkv()

    def arrived(buffer, sent, got, number):
        source = att_out.at[0] if buffer is not dkv else dkv_out.at[0]
        remote(source, buffer.at[number], sent.at[0], got.at[number], twin).wait_recv()

    for oz in column:
        number = oz * view + w
        arrived(dq, dq_s, dq_r, number)
        start(twin_copy(dq.at[number], dq, dq_s.at[pts + oz], dq_r, number))
    for oz in column:
        number = oz * view + w
        arrived(att, att_s, att_r, number)
        start(twin_copy(att.at[number], att, att_s.at[pts + oz], att_r, number))
    for other, _, _ in others:
        arrived(dkv, dkv_s, dkv_r, other)
    for oz in range(pts):
        number = oz * view + lax.rem(w + 1, view)
        arrived(dq, dq_s, dq_r, number)
        arrived(att, att_s, att_r, number)
    for oz in column:
        dq_copy(oz).wait_send()
    for copy in sends:
        copy.wait_send()
    for copy in kept:
        copy.wait()


def unpack_kernel(att, dq, dkv, att_hbm, dq_hbm, dk_hbm, dv_hbm, att_ref, dq_ref, dk_ref, dv_ref, sems):
    peers = att.shape[0]
    half_rows = att.shape[1]

    def write(source, target, number):
        copy = pltpu.make_async_copy(source, target, sems.at[number])
        copy.start()
        return copy

    def two(buffer, pair, side):
        at = slice(side * DH, (side + 1) * DH)
        return jnp.concatenate([buffer[2 * pair][:, at], buffer[2 * pair + 1][:, at]], axis=1)

    copies = []
    for number, (buffer, ref, out) in enumerate(((att, att_ref, att_hbm), (dq, dq_ref, dq_hbm))):
        for pair in range(peers // 2):
            cols = slice(pair * WIDE, (pair + 1) * WIDE)
            ref[:half_rows, cols] = two(buffer, pair, 0)
            ref[half_rows:, cols] = two(buffer, pair, 1)
        copies.append(write(ref, out, number))
    for side, (ref, out) in enumerate(((dk_ref, dk_hbm), (dv_ref, dv_hbm))):
        for pair in range(peers // 2):
            cols = slice(pair * WIDE, (pair + 1) * WIDE)
            ref[:, cols] = two(dkv, pair, side)
        copies.append(write(ref, out, 2 + side))
    for copy in copies:
        copy.wait()


def by_head(queries, key_tiles, value_tiles, visible, destination, d_out):
    pts = lax.axis_size("pts")
    view = lax.axis_size("view")
    peers = pts * view
    kv_dev, tile_keys, width = key_tiles.shape
    held = kv_dev * tile_keys
    p_dev = queries.shape[0]
    keys = peers * held
    whole = pl.BlockSpec(memory_space=pltpu.VMEM)
    bf = jnp.bfloat16
    dma = pltpu.SemaphoreType.DMA
    anywhere = pl.BlockSpec(memory_space=pltpu.HBM)
    vmem = pltpu.VMEM
    operands = (
        queries,
        key_tiles.reshape(held, width),
        value_tiles.reshape(held, width),
        visible,
        destination.reshape(p_dev // WIDE, WIDE),
        d_out,
    )
    landed = (
        jax.ShapeDtypeStruct((peers, p_dev // 2, WIDE), bf),
        jax.ShapeDtypeStruct((peers, p_dev // 2, WIDE), bf),
        jax.ShapeDtypeStruct((peers, held, WIDE), bf),
    )
    att, dq, dkv = pl.pallas_call(
        functools.partial(head_kernel, pts, view),
        out_shape=landed,
        in_specs=[anywhere] * 6,
        out_specs=(anywhere,) * 3,
        scratch_shapes=[vmem(x.shape, x.dtype) for x in operands]
        + [
            vmem((peers, META_ROWS, WIDE), jnp.int32),
            vmem((peers, held, WIDE), bf),
            vmem((peers, held, WIDE), bf),
            vmem((pts, p_dev, WIDE), bf),
            vmem((pts, p_dev, WIDE), bf),
            vmem((pts, META_ROWS, keys), jnp.float32),
            vmem((pts * p_dev, pts * p_dev), bf),
            vmem((pts, p_dev, WIDE), bf),
            vmem((WIDE, keys), jnp.float32),
            vmem((pts, p_dev // 2, WIDE), bf),
            vmem((pts, p_dev // 2, WIDE), bf),
            vmem((peers, held, WIDE), bf),
            dma((6,)),
            dma((peers,)),
            dma((peers,)),
            dma((peers,)),
            dma((peers,)),
            dma((pts,)),
            dma((pts,)),
            dma((2 * pts,)),
            dma((peers,)),
            dma((2 * pts,)),
            dma((peers,)),
            dma((peers,)),
            dma((peers,)),
        ],
        compiler_params=pltpu.CompilerParams(
            collective_id=0, has_side_effects=True, vmem_limit_bytes=ROOM
        ),
        cost_estimate=pl.CostEstimate(
            flops=14 * pts * p_dev * keys * DH,
            bytes_accessed=6 * p_dev * width * 2,
            transcendentals=pts * p_dev * keys,
        ),
    )(*operands)
    finals = [(p_dev, width), (p_dev, width), (held, width), (held, width)]
    attended, d_queries, d_keys, d_values = pl.pallas_call(
        unpack_kernel,
        out_shape=tuple(jax.ShapeDtypeStruct(shape, bf) for shape in finals),
        in_specs=[whole] * 3,
        out_specs=(anywhere,) * 4,
        scratch_shapes=[vmem(shape, bf) for shape in finals] + [dma((4,))],
    )(att, dq, dkv)
    return (
        attended,
        d_queries,
        d_keys.reshape(key_tiles.shape),
        d_values.reshape(value_tiles.shape),
    )


def solution(mesh):
    in_specs = (
        P(("scene", "pts"), "head"),
        P(("scene", "pts", "view"), None, "head"),
        P(("scene", "pts", "view"), None, "head"),
        P(("scene", "pts"), "view"),
        P(("scene", "pts")),
        P(("scene", "pts"), "head"),
    )
    out_specs = (
        P(("scene", "pts"), "head"),
        P(("scene", "pts"), "head"),
        P(("scene", "pts", "view"), None, "head"),
        P(("scene", "pts", "view"), None, "head"),
    )
    heads_local = HEADS // mesh.shape["head"]
    per_device = local
    if heads_local == mesh.shape["pts"] * mesh.shape["view"] and mesh.shape["view"] == 2:
        per_device = by_head
    return jax.shard_map(per_device, mesh=mesh, in_specs=in_specs, out_specs=out_specs, check_vma=False)
```

```python
import functools
import math

import jax
import jax.numpy as jnp
from jax import lax
from jax.experimental import pallas as pl
from jax.experimental.pallas import tpu as pltpu
from jax.sharding import PartitionSpec as P

DH = 64
HEADS = 16
DIST = 32


HIGHEST = lax.Precision.HIGHEST


def merged(value, axis, join):
    pieces = jax.tree.map(lambda part: lax.all_gather(part, axis), value)
    head = jax.tree.map(lambda part: part[0], pieces)
    tail = jax.tree.map(lambda part: part[1:], pieces)
    running, _ = lax.scan(lambda running, share: (join(running, share), None), head, tail)
    return running


def pick(table, ids):
    hits = (ids.reshape(-1)[:, None] == jnp.arange(table.shape[0])[None, :]).astype(jnp.bfloat16)
    flat = jnp.dot(
        hits, table.reshape(table.shape[0], -1), preferred_element_type=jnp.float32
    ).astype(table.dtype)
    return flat.reshape(ids.shape + table.shape[1:])


def fetch_tiles(requests, key_tiles, value_tiles):
    asked_ids = lax.all_to_all(requests, "pts", split_axis=0, concat_axis=0, tiled=True)
    safe_ids = jnp.maximum(asked_ids, 0)
    keys_out = pick(key_tiles, safe_ids)
    values_out = pick(value_tiles, safe_ids)
    keys_back = lax.all_to_all(keys_out, "pts", split_axis=0, concat_axis=0, tiled=True)
    values_back = lax.all_to_all(values_out, "pts", split_axis=0, concat_axis=0, tiled=True)
    return (keys_back, values_back, asked_ids)


def refetch_tiles(requests, key_tiles, value_tiles):
    safe_ids = jnp.maximum(
        lax.all_to_all(requests, "pts", split_axis=0, concat_axis=0, tiled=True), 0
    )
    keys_out = pick(key_tiles, safe_ids)
    values_out = pick(value_tiles, safe_ids)
    return (
        lax.all_to_all(keys_out, "pts", split_axis=0, concat_axis=0, tiled=True),
        lax.all_to_all(values_out, "pts", split_axis=0, concat_axis=0, tiled=True),
    )


def widen(stats):
    return jnp.repeat(stats, DH, axis=1)


def local(queries, key_tiles, value_tiles, visible, destination, d_out):
    pts_count = lax.axis_size("pts")
    view_count = lax.axis_size("view")
    kv_dev, tile_keys, local_width = key_tiles.shape
    qb_dev, nvis = visible.shape
    p_dev = queries.shape[0]
    qblock = p_dev // qb_dev
    heads_local = local_width // DH
    group_heads = math.gcd(heads_local, 4)
    group_width = group_heads * DH
    group_total = heads_local // group_heads
    capacity = max(2, min(kv_dev, 2 * DIST // pts_count))
    score_scale = DH ** (-0.5)
    slot_total = pts_count * capacity
    entries = visible.reshape(-1)
    entry_count = entries.shape[0]
    owner_of = entries // kv_dev // view_count
    local_id = entries % kv_dev
    positions = jnp.arange(entry_count)
    same_id = entries[:, None] == entries[None, :]
    earlier = positions[None, :] < positions[:, None]
    first_seen = jnp.logical_not(jnp.any(same_id & earlier, axis=1))
    same_owner = (owner_of[:, None] == owner_of[None, :]) & earlier & first_seen[None, :]
    owner_rank = jnp.sum(same_owner.astype(jnp.int32), axis=1)
    own_slot = owner_of * capacity + owner_rank
    slot_of = jnp.sum(jnp.where(same_id & first_seen[None, :], own_slot[None, :], 0), axis=1)
    slot_grid = jnp.arange(slot_total)
    slot_hit = (own_slot[None, :] == slot_grid[:, None]) & first_seen[None, :]
    requests = (jnp.sum(jnp.where(slot_hit, local_id[None, :] + 1, 0), axis=1) - 1).reshape(
        pts_count, capacity
    )
    slot_table = slot_of.reshape(qb_dev, nvis)

    def block_tiles(fetched):
        flat_tiles = fetched.reshape(slot_total, tile_keys, local_width)
        return pick(flat_tiles, slot_table).reshape(
            qb_dev, nvis * tile_keys, local_width
        )

    fetched_keys, fetched_values, asked = fetch_tiles(requests, key_tiles, value_tiles)
    block_keys = block_tiles(fetched_keys)
    block_values = block_tiles(fetched_values)
    query_blocks = queries.reshape(qb_dev, qblock, local_width)
    key_count = nvis * tile_keys
    peak_list, total_list, weighted_list = ([], [], [])
    for group_number in range(group_total):
        col_start = group_number * group_width
        col_stop = col_start + group_width
        query_part = query_blocks[..., col_start:col_stop].reshape(qb_dev, qblock, group_heads, DH)
        key_part = block_keys[..., col_start:col_stop].reshape(qb_dev, key_count, group_heads, DH)
        value_part = block_values[..., col_start:col_stop].reshape(
            qb_dev, key_count, group_heads, DH
        )
        scores = (
            jnp.einsum("bqhd,bkhd->bhqk", query_part, key_part, preferred_element_type=jnp.float32)
            * score_scale
        )
        local_peak = jnp.max(scores, axis=-1)
        exponent = jnp.exp(scores - local_peak[..., None])
        local_total = jnp.sum(exponent, axis=-1)
        weighted = jnp.einsum(
            "bhqk,bkhd->bqhd",
            exponent.astype(jnp.bfloat16),
            value_part,
            preferred_element_type=jnp.float32,
        )
        peak_list.append(jnp.transpose(local_peak, (0, 2, 1)))
        total_list.append(jnp.transpose(local_total, (0, 2, 1)))
        weighted_list.append(weighted.reshape(qb_dev, qblock, group_width))
    peak_rows = jnp.concatenate(peak_list, axis=-1).reshape(p_dev, heads_local)
    total_rows = jnp.concatenate(total_list, axis=-1).reshape(p_dev, heads_local)
    weighted_rows = jnp.concatenate(weighted_list, axis=-1).reshape(p_dev, local_width)

    def join(first_part, second_part):
        peak_a, total_a, sum_a = first_part
        peak_b, total_b, sum_b = second_part
        peak_top = jnp.maximum(peak_a, peak_b)
        factor_a = jnp.exp(peak_a - peak_top)
        factor_b = jnp.exp(peak_b - peak_top)
        return (
            peak_top,
            factor_a * total_a + factor_b * total_b,
            widen(factor_a) * sum_a + widen(factor_b) * sum_b,
        )

    big_peak, big_total, big_sum = merged((peak_rows, total_rows, weighted_rows), "view", join)
    attended_rows = (big_sum / widen(big_total)).astype(jnp.bfloat16)
    again_keys, again_values = refetch_tiles(requests, key_tiles, value_tiles)
    grad_keys = block_tiles(again_keys)
    grad_values = block_tiles(again_values)
    delta_rows = jnp.sum(
        (d_out.astype(jnp.float32) * attended_rows.astype(jnp.float32)).reshape(
            p_dev, heads_local, DH
        ),
        axis=-1,
    )
    peak_heads = big_peak.reshape(qb_dev, qblock, heads_local)
    total_heads = big_total.reshape(qb_dev, qblock, heads_local)
    delta_heads = delta_rows.reshape(qb_dev, qblock, heads_local)
    grad_blocks = d_out.reshape(qb_dev, qblock, local_width)
    dquery_list, dkey_list, dvalue_list = ([], [], [])
    for group_number in range(group_total):
        col_start = group_number * group_width
        col_stop = col_start + group_width
        head_start = group_number * group_heads
        head_stop = head_start + group_heads
        query_part = query_blocks[..., col_start:col_stop].reshape(qb_dev, qblock, group_heads, DH)
        key_part = grad_keys[..., col_start:col_stop].reshape(qb_dev, key_count, group_heads, DH)
        value_part = grad_values[..., col_start:col_stop].reshape(
            qb_dev, key_count, group_heads, DH
        )
        grad_part = grad_blocks[..., col_start:col_stop].reshape(qb_dev, qblock, group_heads, DH)
        peak_part = jnp.transpose(peak_heads[..., head_start:head_stop], (0, 2, 1))[..., None]
        total_part = jnp.transpose(total_heads[..., head_start:head_stop], (0, 2, 1))[..., None]
        delta_part = jnp.transpose(delta_heads[..., head_start:head_stop], (0, 2, 1))[..., None]
        scores = (
            jnp.einsum("bqhd,bkhd->bhqk", query_part, key_part, preferred_element_type=jnp.float32)
            * score_scale
        )
        probability = jnp.exp(scores - peak_part) / total_part
        value_grad = jnp.einsum(
            "bhqk,bqhd->bkhd",
            probability.astype(jnp.bfloat16),
            grad_part,
            preferred_element_type=jnp.float32,
        )
        d_prob = jnp.einsum(
            "bqhd,bkhd->bhqk", grad_part, value_part, preferred_element_type=jnp.float32
        )
        d_score = (probability * (d_prob - delta_part)).astype(jnp.bfloat16)
        query_grad = (
            jnp.einsum("bhqk,bkhd->bqhd", d_score, key_part, preferred_element_type=jnp.float32)
            * score_scale
        )
        key_grad = (
            jnp.einsum("bhqk,bqhd->bkhd", d_score, query_part, preferred_element_type=jnp.float32)
            * score_scale
        )
        dquery_list.append(query_grad.reshape(qb_dev, qblock, group_width))
        dkey_list.append(key_grad.reshape(qb_dev, key_count, group_width))
        dvalue_list.append(value_grad.reshape(qb_dev, key_count, group_width))
    dquery_local = jnp.concatenate(dquery_list, axis=-1).reshape(p_dev, local_width)
    dkey_blocks = jnp.concatenate(dkey_list, axis=-1)
    dvalue_blocks = jnp.concatenate(dvalue_list, axis=-1)
    d_queries = lax.psum(dquery_local, "view").astype(jnp.bfloat16)
    slot_match = (slot_of[None, :] == slot_grid[:, None]).astype(jnp.float32)

    def per_slot(blocks):
        flat_rows = blocks.reshape(qb_dev * nvis, tile_keys * local_width)
        summed = jnp.dot(
            slot_match, flat_rows, precision=HIGHEST, preferred_element_type=jnp.float32
        )
        return summed.astype(jnp.bfloat16).reshape(pts_count, capacity, tile_keys, local_width)

    back_keys, back_values = (
        lax.all_to_all(per_slot(dkey_blocks), "pts", split_axis=0, concat_axis=0, tiled=True),
        lax.all_to_all(per_slot(dvalue_blocks), "pts", split_axis=0, concat_axis=0, tiled=True),
    )
    owner_match = (asked.reshape(-1)[None, :] == jnp.arange(kv_dev)[:, None]).astype(jnp.bfloat16)
    d_keys = (
        jnp.dot(
            owner_match,
            back_keys.reshape(slot_total, tile_keys * local_width),
            preferred_element_type=jnp.float32,
        )
        .astype(jnp.bfloat16)
        .reshape(kv_dev, tile_keys, local_width)
    )
    d_values = (
        jnp.dot(
            owner_match,
            back_values.reshape(slot_total, tile_keys * local_width),
            preferred_element_type=jnp.float32,
        )
        .astype(jnp.bfloat16)
        .reshape(kv_dev, tile_keys, local_width)
    )
    per_peer = p_dev // pts_count
    target = destination // p_dev
    row_place = destination % p_dev
    peer_hits = (target[:, None] == jnp.arange(pts_count)[None, :]).astype(jnp.int32)
    ahead = jnp.arange(p_dev)[None, :] < jnp.arange(p_dev)[:, None]
    before = jnp.dot(
        ahead.astype(jnp.bfloat16),
        peer_hits.astype(jnp.bfloat16),
        preferred_element_type=jnp.float32,
    ).astype(jnp.int32)
    send_rank = jnp.sum(before * peer_hits, axis=1)
    send_position = target * per_peer + send_rank
    row_numbers = jnp.arange(p_dev, dtype=jnp.int32)
    send_inverse = jnp.zeros((p_dev,), jnp.int32).at[send_position].set(row_numbers)
    rows_out = attended_rows[send_inverse].reshape(pts_count, per_peer, local_width)
    places_out = row_place[send_inverse].reshape(pts_count, per_peer)
    got_rows, got_places = (
        lax.all_to_all(rows_out, "pts", split_axis=0, concat_axis=0, tiled=True),
        lax.all_to_all(places_out, "pts", split_axis=0, concat_axis=0, tiled=True),
    )
    place_inverse = jnp.zeros((p_dev,), jnp.int32).at[got_places.reshape(-1)].set(row_numbers)
    attended = got_rows.reshape(p_dev, local_width)[place_inverse]
    return (attended, d_queries, d_keys, d_values)


MESH = pl.DeviceIdType.MESH
WIDE = 2 * DH
TILE = 16
HIDDEN = -1e30
ROOM = 63 * 1024 * 1024
META_ROWS = 8


def partner(z, step, pts):
    found, unit = 0, 1
    while unit < pts:
        found = found + unit * lax.rem(z // unit + step // unit, 2)
        unit *= 2
    return found


def remote(src, dst, send_sem, recv_sem, place):
    return pltpu.make_async_remote_copy(
        src_ref=src,
        dst_ref=dst,
        send_sem=send_sem,
        recv_sem=recv_sem,
        device_id=place,
        device_id_type=MESH,
    )


def head_kernel(
    pts,
    view,
    q_hbm,
    k_hbm,
    v_hbm,
    vis_hbm,
    dest_hbm,
    g_hbm,
    att,
    dq,
    dkv,
    q_ref,
    k_ref,
    v_ref,
    vis_ref,
    dest_ref,
    g_ref,
    meta,
    kv_out,
    kv,
    qd_out,
    qd,
    bias,
    place,
    rows,
    grads,
    att_out,
    dq_out,
    dkv_out,
    load_s,
    meta_s,
    meta_r,
    kv_s,
    kv_r,
    qd_s,
    qd_r,
    att_s,
    att_r,
    dq_s,
    dq_r,
    dkv_s,
    dkv_r,
):
    z = lax.axis_index("pts")
    w = lax.axis_index("view")
    peers = pts * view
    me = z * view + w
    p_dev = q_ref.shape[0]
    qb_dev, nvis = vis_ref.shape
    qblock = p_dev // qb_dev
    held = k_ref.shape[0]
    keys = peers * held
    dest_rows = dest_ref.shape[0]

    barrier = pltpu.get_barrier_semaphore()
    others = []
    for step in range(1, peers):
        other = lax.rem(me + step, peers)
        others.append((other, other // view, lax.rem(other, view)))
    column = []
    for step in range(1, pts):
        column.append(partner(z, step, pts))
    for _, oz, ow in others:
        pl.semaphore_signal(barrier, inc=1, device_id={"pts": oz, "view": ow}, device_id_type=MESH)

    loads = []
    pairs = (
        (k_hbm, k_ref),
        (v_hbm, v_ref),
        (vis_hbm, vis_ref),
        (dest_hbm, dest_ref),
        (q_hbm, q_ref),
        (g_hbm, g_ref),
    )
    for number, (source, target) in enumerate(pairs):
        load = pltpu.make_async_copy(source, target, load_s.at[number])
        load.start()
        loads.append(load)
    meta[me] = jnp.zeros((META_ROWS, WIDE), jnp.int32)
    for load in loads[:4]:
        load.wait()
    meta[me, 0:qb_dev, 0:nvis] = vis_ref[...]
    meta[me, qb_dev : qb_dev + dest_rows, :] = dest_ref[...]
    for pair in range(peers // 2):
        cols = slice(pair * WIDE, (pair + 1) * WIDE)
        kt, vt = k_ref[:, cols], v_ref[:, cols]
        kv_out[2 * pair] = jnp.concatenate([kt[:, :DH], vt[:, :DH]], axis=1)
        kv_out[2 * pair + 1] = jnp.concatenate([kt[:, DH:], vt[:, DH:]], axis=1)
    pl.semaphore_wait(barrier, peers - 1)

    sends = []

    def start(copy):
        copy.start()
        sends.append(copy)

    for other, oz, ow in others:
        spot = {"pts": oz, "view": ow}
        start(remote(meta.at[me], meta.at[me], meta_s.at[other], meta_r.at[me], spot))
    for other, oz, ow in others:
        spot = {"pts": oz, "view": ow}
        start(remote(kv_out.at[other], kv.at[me], kv_s.at[other], kv_r.at[me], spot))
    kv[me] = kv_out[me]
    for load in loads[4:]:
        load.wait()

    for peer in range(pts):
        parts = []
        for half in range(view):
            at = (peer * view + half) * DH
            tile = (at // WIDE) * WIDE
            off = at - tile
            parts.append((q_ref[:, tile + off : tile + off + DH], g_ref[:, tile + off : tile + off + DH]))
        qh, gh = parts[0]
        packed = jnp.concatenate([qh, gh], axis=1)
        for half in range(1, view):
            qn, gn = parts[half]
            packed = jnp.where(w == half, jnp.concatenate([qn, gn], axis=1), packed)
        qd_out[peer] = packed
    for oz in column:
        spot = {"pts": oz, "view": w}
        start(remote(qd_out.at[oz], qd.at[z], qd_s.at[oz], qd_r.at[z], spot))
    qd[z] = qd_out[z]

    for other, oz, ow in others:
        remote(meta.at[me], meta.at[other], meta_s.at[other], meta_r.at[other], {"pts": oz, "view": ow}).wait_recv()

    tile_of = lax.broadcasted_iota(jnp.int32, (META_ROWS, keys), 1) // (keys // (peers * (held // TILE)))
    for p in range(pts):
        hit = None
        for half in range(view):
            ids = meta[p * view + half]
            for i in range(nvis):
                one = ids[:, i : i + 1] == tile_of
                hit = one if hit is None else hit | one
        bias[p] = jnp.where(hit, 0.0, HIDDEN)
    row_number = lax.broadcasted_iota(jnp.int32, (pts * p_dev, WIDE), 0)
    for p in range(pts):
        for c in range(dest_rows):
            line = meta[p * view, qb_dev + c : qb_dev + c + 1, :]
            at = p * p_dev + c * WIDE
            place[:, at : at + WIDE] = jnp.where(row_number == line, 1.0, 0.0).astype(jnp.bfloat16)

    for other, oz, ow in others:
        remote(kv_out.at[0], kv.at[other], kv_s.at[other], kv_r.at[other], {"pts": oz, "view": ow}).wait_recv()
    grads[...] = jnp.zeros_like(grads)

    lower = lax.broadcasted_iota(jnp.int32, (p_dev, WIDE), 1) < DH
    zero = jnp.zeros((), jnp.bfloat16)
    scale = DH**-0.5
    nt = (((1,), (1,)), ((), ()))

    def shade(p):
        lines = [jnp.broadcast_to(bias[p, b : b + 1, :], (qblock, keys)) for b in range(qb_dev)]
        return jnp.concatenate(lines, axis=0)

    def block(p):
        both = kv[...].reshape(keys, WIDE)
        mixed = qd[p]
        query = jnp.where(lower, mixed * jnp.asarray(scale, jnp.bfloat16), zero)
        grad = jnp.where(lower, zero, mixed)
        scores = lax.dot_general(query, both, nt, preferred_element_type=jnp.float32)
        scores = scores + shade(p)
        d_prob = lax.dot_general(grad, both, nt, preferred_element_type=jnp.float32)
        peak = jnp.max(scores, axis=1, keepdims=True)
        weight = jnp.exp(scores - peak)
        total = jnp.sum(weight, axis=1, keepdims=True)
        inverse = 1.0 / total
        summed = jnp.dot(weight.astype(jnp.bfloat16), both, preferred_element_type=jnp.float32)
        out = (summed / total).astype(jnp.bfloat16)
        delta = jnp.sum(
            grad.astype(jnp.float32) * out.astype(jnp.float32), axis=1, keepdims=True
        )
        prob = weight * inverse
        d_score = (prob * (d_prob - delta)).astype(jnp.bfloat16)
        d_query = jnp.dot(d_score, both, preferred_element_type=jnp.float32) * scale
        left = jnp.concatenate([query, grad], axis=0)
        right = jnp.concatenate([d_score, prob.astype(jnp.bfloat16)], axis=0)
        grads[...] += jnp.dot(left.T, right, preferred_element_type=jnp.float32)
        return jnp.where(lower, d_query.astype(jnp.bfloat16), out)

    half_rows = p_dev // 2
    twin = {"pts": z, "view": lax.rem(w + 1, view)}

    def fold(upper, lower_half, side):
        at = slice(side * DH, (side + 1) * DH)
        return jnp.concatenate([upper[:, at], lower_half[:, at]], axis=1)

    def dq_copy(p):
        spot = {"pts": p, "view": w}
        return remote(dq_out.at[p], dq.at[me], dq_s.at[p], dq_r.at[me], spot)

    def twin_copy(source, target, sent, got, number):
        return remote(source, target.at[number], sent, got.at[number], twin)

    def step_body(step, carry):
        p = partner(z, step, pts)

        if step > 0:
            remote(qd_out.at[0], qd.at[p], qd_s.at[p], qd_r.at[p], {"pts": p, "view": w}).wait_recv()

        rows[p] = block(p)
        dq_out[p] = fold(rows[p, :half_rows, :], rows[p, half_rows:, :], 0)

        if step > 0:
            dq_copy(p).start()

        return carry

    for step in range(pts):
        step_body(step, 0)
    kept = []
    start(twin_copy(dq_out.at[z], dq, dq_s.at[z], dq_r, me))
    dq_own = pltpu.make_async_copy(dq_out.at[z], dq.at[me], load_s.at[0])
    dq_own.start()
    kept.append(dq_own)

    def send_att():
        every = rows[...].reshape(pts * p_dev, WIDE)
        moved = jnp.dot(place[...], every, preferred_element_type=jnp.float32)
        for p in range(pts):
            top = moved[p * p_dev : p * p_dev + half_rows]
            low = moved[p * p_dev + half_rows : (p + 1) * p_dev]
            att_out[p] = fold(top, low, 1).astype(jnp.bfloat16)
        for oz in column:
            spot = {"pts": oz, "view": w}
            start(remote(att_out.at[oz], att.at[me], att_s.at[oz], att_r.at[me], spot))
        start(twin_copy(att_out.at[z], att, att_s.at[z], att_r, me))
        att_own = pltpu.make_async_copy(att_out.at[z], att.at[me], load_s.at[1])
        att_own.start()
        kept.append(att_own)

    def send_dkv():
        dkv_out[...] = grads[...].T.astype(jnp.bfloat16).reshape(dkv_out.shape)
        for other, oz, ow in others:
            spot = {"pts": oz, "view": ow}
            start(remote(dkv_out.at[other], dkv.at[me], dkv_s.at[other], dkv_r.at[me], spot))
        dkv_own = pltpu.make_async_copy(dkv_out.at[me], dkv.at[me], load_s.at[2])
        dkv_own.start()
        kept.append(dkv_own)

    send_att()
    send_dkv()

    def arrived(buffer, sent, got, number):
        source = att_out.at[0] if buffer is not dkv else dkv_out.at[0]
        remote(source, buffer.at[number], sent.at[0], got.at[number], twin).wait_recv()

    for oz in column:
        number = oz * view + w
        arrived(dq, dq_s, dq_r, number)
        start(twin_copy(dq.at[number], dq, dq_s.at[pts + oz], dq_r, number))
    for oz in column:
        number = oz * view + w
        arrived(att, att_s, att_r, number)
        start(twin_copy(att.at[number], att, att_s.at[pts + oz], att_r, number))
    for other, _, _ in others:
        arrived(dkv, dkv_s, dkv_r, other)
    for oz in range(pts):
        number = oz * view + lax.rem(w + 1, view)
        arrived(dq, dq_s, dq_r, number)
        arrived(att, att_s, att_r, number)
    for oz in column:
        dq_copy(oz).wait_send()
    for copy in sends:
        copy.wait_send()
    for copy in kept:
        copy.wait()


def unpack_kernel(att, dq, dkv, att_hbm, dq_hbm, dk_hbm, dv_hbm, att_ref, dq_ref, dk_ref, dv_ref, sems):
    peers = att.shape[0]
    half_rows = att.shape[1]

    def write(source, target, number):
        copy = pltpu.make_async_copy(source, target, sems.at[number])
        copy.start()
        return copy

    def two(buffer, pair, side):
        at = slice(side * DH, (side + 1) * DH)
        return jnp.concatenate([buffer[2 * pair][:, at], buffer[2 * pair + 1][:, at]], axis=1)

    copies = []
    for number, (buffer, ref, out) in enumerate(((att, att_ref, att_hbm), (dq, dq_ref, dq_hbm))):
        for pair in range(peers // 2):
            cols = slice(pair * WIDE, (pair + 1) * WIDE)
            ref[:half_rows, cols] = two(buffer, pair, 0)
            ref[half_rows:, cols] = two(buffer, pair, 1)
        copies.append(write(ref, out, number))
    for side, (ref, out) in enumerate(((dk_ref, dk_hbm), (dv_ref, dv_hbm))):
        for pair in range(peers // 2):
            cols = slice(pair * WIDE, (pair + 1) * WIDE)
            ref[:, cols] = two(dkv, pair, side)
        copies.append(write(ref, out, 2 + side))
    for copy in copies:
        copy.wait()


def by_head(queries, key_tiles, value_tiles, visible, destination, d_out):
    pts = lax.axis_size("pts")
    view = lax.axis_size("view")
    peers = pts * view
    kv_dev, tile_keys, width = key_tiles.shape
    held = kv_dev * tile_keys
    p_dev = queries.shape[0]
    keys = peers * held
    whole = pl.BlockSpec(memory_space=pltpu.VMEM)
    bf = jnp.bfloat16
    dma = pltpu.SemaphoreType.DMA
    anywhere = pl.BlockSpec(memory_space=pltpu.HBM)
    vmem = pltpu.VMEM
    operands = (
        queries,
        key_tiles.reshape(held, width),
        value_tiles.reshape(held, width),
        visible,
        destination.reshape(p_dev // WIDE, WIDE),
        d_out,
    )
    landed = (
        jax.ShapeDtypeStruct((peers, p_dev // 2, WIDE), bf),
        jax.ShapeDtypeStruct((peers, p_dev // 2, WIDE), bf),
        jax.ShapeDtypeStruct((peers, held, WIDE), bf),
    )
    att, dq, dkv = pl.pallas_call(
        functools.partial(head_kernel, pts, view),
        out_shape=landed,
        in_specs=[anywhere] * 6,
        out_specs=(anywhere,) * 3,
        scratch_shapes=[vmem(x.shape, x.dtype) for x in operands]
        + [
            vmem((peers, META_ROWS, WIDE), jnp.int32),
            vmem((peers, held, WIDE), bf),
            vmem((peers, held, WIDE), bf),
            vmem((pts, p_dev, WIDE), bf),
            vmem((pts, p_dev, WIDE), bf),
            vmem((pts, META_ROWS, keys), jnp.float32),
            vmem((pts * p_dev, pts * p_dev), bf),
            vmem((pts, p_dev, WIDE), bf),
            vmem((WIDE, keys), jnp.float32),
            vmem((pts, p_dev // 2, WIDE), bf),
            vmem((pts, p_dev // 2, WIDE), bf),
            vmem((peers, held, WIDE), bf),
            dma((6,)),
            dma((peers,)),
            dma((peers,)),
            dma((peers,)),
            dma((peers,)),
            dma((pts,)),
            dma((pts,)),
            dma((2 * pts,)),
            dma((peers,)),
            dma((2 * pts,)),
            dma((peers,)),
            dma((peers,)),
            dma((peers,)),
        ],
        compiler_params=pltpu.CompilerParams(
            collective_id=0, has_side_effects=True, vmem_limit_bytes=ROOM
        ),
        cost_estimate=pl.CostEstimate(
            flops=14 * pts * p_dev * keys * DH,
            bytes_accessed=6 * p_dev * width * 2,
            transcendentals=pts * p_dev * keys,
        ),
    )(*operands)
    finals = [(p_dev, width), (p_dev, width), (held, width), (held, width)]
    attended, d_queries, d_keys, d_values = pl.pallas_call(
        unpack_kernel,
        out_shape=tuple(jax.ShapeDtypeStruct(shape, bf) for shape in finals),
        in_specs=[whole] * 3,
        out_specs=(anywhere,) * 4,
        scratch_shapes=[vmem(shape, bf) for shape in finals] + [dma((4,))],
    )(att, dq, dkv)
    return (
        attended,
        d_queries,
        d_keys.reshape(key_tiles.shape),
        d_values.reshape(value_tiles.shape),
    )


def solution(mesh):
    in_specs = (
        P(("scene", "pts"), "head"),
        P(("scene", "pts", "view"), None, "head"),
        P(("scene", "pts", "view"), None, "head"),
        P(("scene", "pts"), "view"),
        P(("scene", "pts")),
        P(("scene", "pts"), "head"),
    )
    out_specs = (
        P(("scene", "pts"), "head"),
        P(("scene", "pts"), "head"),
        P(("scene", "pts", "view"), None, "head"),
        P(("scene", "pts", "view"), None, "head"),
    )
    heads_local = HEADS // mesh.shape["head"]
    per_device = local
    pts = mesh.shape["pts"]
    paired = mesh.shape["view"] == 2 and pts & (pts - 1) == 0
    if paired and heads_local == pts * mesh.shape["view"]:
        per_device = by_head
    return jax.shard_map(per_device, mesh=mesh, in_specs=in_specs, out_specs=out_specs, check_vma=False)
```

```python
import functools
import math

import jax
import jax.numpy as jnp
from jax import lax
from jax.experimental import pallas as pl
from jax.experimental.pallas import tpu as pltpu
from jax.sharding import PartitionSpec as P

DH = 64
HEADS = 16
DIST = 32


HIGHEST = lax.Precision.HIGHEST


def merged(value, axis, join):
    pieces = jax.tree.map(lambda part: lax.all_gather(part, axis), value)
    head = jax.tree.map(lambda part: part[0], pieces)
    tail = jax.tree.map(lambda part: part[1:], pieces)
    running, _ = lax.scan(lambda running, share: (join(running, share), None), head, tail)
    return running


def pick(table, ids):
    hits = (ids.reshape(-1)[:, None] == jnp.arange(table.shape[0])[None, :]).astype(jnp.bfloat16)
    flat = jnp.dot(
        hits, table.reshape(table.shape[0], -1), preferred_element_type=jnp.float32
    ).astype(table.dtype)
    return flat.reshape(ids.shape + table.shape[1:])


def fetch_tiles(requests, key_tiles, value_tiles):
    asked_ids = lax.all_to_all(requests, "pts", split_axis=0, concat_axis=0, tiled=True)
    safe_ids = jnp.maximum(asked_ids, 0)
    keys_out = pick(key_tiles, safe_ids)
    values_out = pick(value_tiles, safe_ids)
    keys_back = lax.all_to_all(keys_out, "pts", split_axis=0, concat_axis=0, tiled=True)
    values_back = lax.all_to_all(values_out, "pts", split_axis=0, concat_axis=0, tiled=True)
    return (keys_back, values_back, asked_ids)


def refetch_tiles(requests, key_tiles, value_tiles):
    safe_ids = jnp.maximum(
        lax.all_to_all(requests, "pts", split_axis=0, concat_axis=0, tiled=True), 0
    )
    keys_out = pick(key_tiles, safe_ids)
    values_out = pick(value_tiles, safe_ids)
    return (
        lax.all_to_all(keys_out, "pts", split_axis=0, concat_axis=0, tiled=True),
        lax.all_to_all(values_out, "pts", split_axis=0, concat_axis=0, tiled=True),
    )


def widen(stats):
    return jnp.repeat(stats, DH, axis=1)


def local(queries, key_tiles, value_tiles, visible, destination, d_out):
    pts_count = lax.axis_size("pts")
    view_count = lax.axis_size("view")
    kv_dev, tile_keys, local_width = key_tiles.shape
    qb_dev, nvis = visible.shape
    p_dev = queries.shape[0]
    qblock = p_dev // qb_dev
    heads_local = local_width // DH
    group_heads = math.gcd(heads_local, 4)
    group_width = group_heads * DH
    group_total = heads_local // group_heads
    capacity = max(2, min(kv_dev, 2 * DIST // pts_count))
    score_scale = DH ** (-0.5)
    slot_total = pts_count * capacity
    entries = visible.reshape(-1)
    entry_count = entries.shape[0]
    owner_of = entries // kv_dev // view_count
    local_id = entries % kv_dev
    positions = jnp.arange(entry_count)
    same_id = entries[:, None] == entries[None, :]
    earlier = positions[None, :] < positions[:, None]
    first_seen = jnp.logical_not(jnp.any(same_id & earlier, axis=1))
    same_owner = (owner_of[:, None] == owner_of[None, :]) & earlier & first_seen[None, :]
    owner_rank = jnp.sum(same_owner.astype(jnp.int32), axis=1)
    own_slot = owner_of * capacity + owner_rank
    slot_of = jnp.sum(jnp.where(same_id & first_seen[None, :], own_slot[None, :], 0), axis=1)
    slot_grid = jnp.arange(slot_total)
    slot_hit = (own_slot[None, :] == slot_grid[:, None]) & first_seen[None, :]
    requests = (jnp.sum(jnp.where(slot_hit, local_id[None, :] + 1, 0), axis=1) - 1).reshape(
        pts_count, capacity
    )
    slot_table = slot_of.reshape(qb_dev, nvis)

    def block_tiles(fetched):
        flat_tiles = fetched.reshape(slot_total, tile_keys, local_width)
        return pick(flat_tiles, slot_table).reshape(
            qb_dev, nvis * tile_keys, local_width
        )

    fetched_keys, fetched_values, asked = fetch_tiles(requests, key_tiles, value_tiles)
    block_keys = block_tiles(fetched_keys)
    block_values = block_tiles(fetched_values)
    query_blocks = queries.reshape(qb_dev, qblock, local_width)
    key_count = nvis * tile_keys
    peak_list, total_list, weighted_list = ([], [], [])
    for group_number in range(group_total):
        col_start = group_number * group_width
        col_stop = col_start + group_width
        query_part = query_blocks[..., col_start:col_stop].reshape(qb_dev, qblock, group_heads, DH)
        key_part = block_keys[..., col_start:col_stop].reshape(qb_dev, key_count, group_heads, DH)
        value_part = block_values[..., col_start:col_stop].reshape(
            qb_dev, key_count, group_heads, DH
        )
        scores = (
            jnp.einsum("bqhd,bkhd->bhqk", query_part, key_part, preferred_element_type=jnp.float32)
            * score_scale
        )
        local_peak = jnp.max(scores, axis=-1)
        exponent = jnp.exp(scores - local_peak[..., None])
        local_total = jnp.sum(exponent, axis=-1)
        weighted = jnp.einsum(
            "bhqk,bkhd->bqhd",
            exponent.astype(jnp.bfloat16),
            value_part,
            preferred_element_type=jnp.float32,
        )
        peak_list.append(jnp.transpose(local_peak, (0, 2, 1)))
        total_list.append(jnp.transpose(local_total, (0, 2, 1)))
        weighted_list.append(weighted.reshape(qb_dev, qblock, group_width))
    peak_rows = jnp.concatenate(peak_list, axis=-1).reshape(p_dev, heads_local)
    total_rows = jnp.concatenate(total_list, axis=-1).reshape(p_dev, heads_local)
    weighted_rows = jnp.concatenate(weighted_list, axis=-1).reshape(p_dev, local_width)

    def join(first_part, second_part):
        peak_a, total_a, sum_a = first_part
        peak_b, total_b, sum_b = second_part
        peak_top = jnp.maximum(peak_a, peak_b)
        factor_a = jnp.exp(peak_a - peak_top)
        factor_b = jnp.exp(peak_b - peak_top)
        return (
            peak_top,
            factor_a * total_a + factor_b * total_b,
            widen(factor_a) * sum_a + widen(factor_b) * sum_b,
        )

    big_peak, big_total, big_sum = merged((peak_rows, total_rows, weighted_rows), "view", join)
    attended_rows = (big_sum / widen(big_total)).astype(jnp.bfloat16)
    again_keys, again_values = refetch_tiles(requests, key_tiles, value_tiles)
    grad_keys = block_tiles(again_keys)
    grad_values = block_tiles(again_values)
    delta_rows = jnp.sum(
        (d_out.astype(jnp.float32) * attended_rows.astype(jnp.float32)).reshape(
            p_dev, heads_local, DH
        ),
        axis=-1,
    )
    peak_heads = big_peak.reshape(qb_dev, qblock, heads_local)
    total_heads = big_total.reshape(qb_dev, qblock, heads_local)
    delta_heads = delta_rows.reshape(qb_dev, qblock, heads_local)
    grad_blocks = d_out.reshape(qb_dev, qblock, local_width)
    dquery_list, dkey_list, dvalue_list = ([], [], [])
    for group_number in range(group_total):
        col_start = group_number * group_width
        col_stop = col_start + group_width
        head_start = group_number * group_heads
        head_stop = head_start + group_heads
        query_part = query_blocks[..., col_start:col_stop].reshape(qb_dev, qblock, group_heads, DH)
        key_part = grad_keys[..., col_start:col_stop].reshape(qb_dev, key_count, group_heads, DH)
        value_part = grad_values[..., col_start:col_stop].reshape(
            qb_dev, key_count, group_heads, DH
        )
        grad_part = grad_blocks[..., col_start:col_stop].reshape(qb_dev, qblock, group_heads, DH)
        peak_part = jnp.transpose(peak_heads[..., head_start:head_stop], (0, 2, 1))[..., None]
        total_part = jnp.transpose(total_heads[..., head_start:head_stop], (0, 2, 1))[..., None]
        delta_part = jnp.transpose(delta_heads[..., head_start:head_stop], (0, 2, 1))[..., None]
        scores = (
            jnp.einsum("bqhd,bkhd->bhqk", query_part, key_part, preferred_element_type=jnp.float32)
            * score_scale
        )
        probability = jnp.exp(scores - peak_part) / total_part
        value_grad = jnp.einsum(
            "bhqk,bqhd->bkhd",
            probability.astype(jnp.bfloat16),
            grad_part,
            preferred_element_type=jnp.float32,
        )
        d_prob = jnp.einsum(
            "bqhd,bkhd->bhqk", grad_part, value_part, preferred_element_type=jnp.float32
        )
        d_score = (probability * (d_prob - delta_part)).astype(jnp.bfloat16)
        query_grad = (
            jnp.einsum("bhqk,bkhd->bqhd", d_score, key_part, preferred_element_type=jnp.float32)
            * score_scale
        )
        key_grad = (
            jnp.einsum("bhqk,bqhd->bkhd", d_score, query_part, preferred_element_type=jnp.float32)
            * score_scale
        )
        dquery_list.append(query_grad.reshape(qb_dev, qblock, group_width))
        dkey_list.append(key_grad.reshape(qb_dev, key_count, group_width))
        dvalue_list.append(value_grad.reshape(qb_dev, key_count, group_width))
    dquery_local = jnp.concatenate(dquery_list, axis=-1).reshape(p_dev, local_width)
    dkey_blocks = jnp.concatenate(dkey_list, axis=-1)
    dvalue_blocks = jnp.concatenate(dvalue_list, axis=-1)
    d_queries = lax.psum(dquery_local, "view").astype(jnp.bfloat16)
    slot_match = (slot_of[None, :] == slot_grid[:, None]).astype(jnp.float32)

    def per_slot(blocks):
        flat_rows = blocks.reshape(qb_dev * nvis, tile_keys * local_width)
        summed = jnp.dot(
            slot_match, flat_rows, precision=HIGHEST, preferred_element_type=jnp.float32
        )
        return summed.astype(jnp.bfloat16).reshape(pts_count, capacity, tile_keys, local_width)

    back_keys, back_values = (
        lax.all_to_all(per_slot(dkey_blocks), "pts", split_axis=0, concat_axis=0, tiled=True),
        lax.all_to_all(per_slot(dvalue_blocks), "pts", split_axis=0, concat_axis=0, tiled=True),
    )
    owner_match = (asked.reshape(-1)[None, :] == jnp.arange(kv_dev)[:, None]).astype(jnp.bfloat16)
    d_keys = (
        jnp.dot(
            owner_match,
            back_keys.reshape(slot_total, tile_keys * local_width),
            preferred_element_type=jnp.float32,
        )
        .astype(jnp.bfloat16)
        .reshape(kv_dev, tile_keys, local_width)
    )
    d_values = (
        jnp.dot(
            owner_match,
            back_values.reshape(slot_total, tile_keys * local_width),
            preferred_element_type=jnp.float32,
        )
        .astype(jnp.bfloat16)
        .reshape(kv_dev, tile_keys, local_width)
    )
    per_peer = p_dev // pts_count
    target = destination // p_dev
    row_place = destination % p_dev
    peer_hits = (target[:, None] == jnp.arange(pts_count)[None, :]).astype(jnp.int32)
    ahead = jnp.arange(p_dev)[None, :] < jnp.arange(p_dev)[:, None]
    before = jnp.dot(
        ahead.astype(jnp.bfloat16),
        peer_hits.astype(jnp.bfloat16),
        preferred_element_type=jnp.float32,
    ).astype(jnp.int32)
    send_rank = jnp.sum(before * peer_hits, axis=1)
    send_position = target * per_peer + send_rank
    row_numbers = jnp.arange(p_dev, dtype=jnp.int32)
    send_inverse = jnp.zeros((p_dev,), jnp.int32).at[send_position].set(row_numbers)
    rows_out = attended_rows[send_inverse].reshape(pts_count, per_peer, local_width)
    places_out = row_place[send_inverse].reshape(pts_count, per_peer)
    got_rows, got_places = (
        lax.all_to_all(rows_out, "pts", split_axis=0, concat_axis=0, tiled=True),
        lax.all_to_all(places_out, "pts", split_axis=0, concat_axis=0, tiled=True),
    )
    place_inverse = jnp.zeros((p_dev,), jnp.int32).at[got_places.reshape(-1)].set(row_numbers)
    attended = got_rows.reshape(p_dev, local_width)[place_inverse]
    return (attended, d_queries, d_keys, d_values)


MESH = pl.DeviceIdType.MESH
WIDE = 2 * DH
TILE = 16
HIDDEN = -1e30
ROOM = 63 * 1024 * 1024
META_ROWS = 8


def partner(z, step, pts):
    found, unit = 0, 1
    while unit < pts:
        found = found + unit * lax.rem(z // unit + step // unit, 2)
        unit *= 2
    return found


def remote(src, dst, send_sem, recv_sem, place):
    return pltpu.make_async_remote_copy(
        src_ref=src,
        dst_ref=dst,
        send_sem=send_sem,
        recv_sem=recv_sem,
        device_id=place,
        device_id_type=MESH,
    )


def head_kernel(
    pts,
    view,
    q_hbm,
    k_hbm,
    v_hbm,
    vis_hbm,
    dest_hbm,
    g_hbm,
    att,
    dq,
    dkv,
    q_ref,
    k_ref,
    v_ref,
    vis_ref,
    dest_ref,
    g_ref,
    meta,
    kv_out,
    kv,
    qd_out,
    qd,
    bias,
    place,
    rows,
    grads,
    att_out,
    dq_out,
    dkv_out,
    load_s,
    meta_s,
    meta_r,
    kv_s,
    kv_r,
    qd_s,
    qd_r,
    att_s,
    att_r,
    dq_s,
    dq_r,
    dkv_s,
    dkv_r,
):
    z = lax.axis_index("pts")
    w = lax.axis_index("view")
    peers = pts * view
    me = z * view + w
    p_dev = q_ref.shape[0]
    qb_dev, nvis = vis_ref.shape
    qblock = p_dev // qb_dev
    held = k_ref.shape[0]
    keys = peers * held
    dest_rows = dest_ref.shape[0]

    barrier = pltpu.get_barrier_semaphore()
    others = []
    for step in range(1, peers):
        other = partner(me, peers - step, peers)
        others.append((other, other // view, lax.rem(other, view)))
    column = []
    for step in range(1, pts):
        column.append(partner(z, step, pts))
    for _, oz, ow in others:
        pl.semaphore_signal(barrier, inc=1, device_id={"pts": oz, "view": ow}, device_id_type=MESH)

    loads = []
    pairs = (
        (k_hbm, k_ref),
        (v_hbm, v_ref),
        (vis_hbm, vis_ref),
        (dest_hbm, dest_ref),
        (q_hbm, q_ref),
        (g_hbm, g_ref),
    )
    for number, (source, target) in enumerate(pairs):
        load = pltpu.make_async_copy(source, target, load_s.at[number])
        load.start()
        loads.append(load)
    meta[me] = jnp.zeros((META_ROWS, WIDE), jnp.int32)
    for load in loads[:4]:
        load.wait()
    meta[me, 0:qb_dev, 0:nvis] = vis_ref[...]
    meta[me, qb_dev : qb_dev + dest_rows, :] = dest_ref[...]
    for pair in range(peers // 2):
        cols = slice(pair * WIDE, (pair + 1) * WIDE)
        kt, vt = k_ref[:, cols], v_ref[:, cols]
        kv_out[2 * pair] = jnp.concatenate([kt[:, :DH], vt[:, :DH]], axis=1)
        kv_out[2 * pair + 1] = jnp.concatenate([kt[:, DH:], vt[:, DH:]], axis=1)
    pl.semaphore_wait(barrier, peers - 1)

    sends = []

    def start(copy):
        copy.start()
        sends.append(copy)

    for other, oz, ow in others:
        spot = {"pts": oz, "view": ow}
        start(remote(meta.at[me], meta.at[me], meta_s.at[other], meta_r.at[me], spot))
    for other, oz, ow in others:
        spot = {"pts": oz, "view": ow}
        start(remote(kv_out.at[other], kv.at[me], kv_s.at[other], kv_r.at[me], spot))
    kv[me] = kv_out[me]
    for load in loads[4:]:
        load.wait()

    for peer in range(pts):
        parts = []
        for half in range(view):
            at = (peer * view + half) * DH
            tile = (at // WIDE) * WIDE
            off = at - tile
            parts.append((q_ref[:, tile + off : tile + off + DH], g_ref[:, tile + off : tile + off + DH]))
        qh, gh = parts[0]
        packed = jnp.concatenate([qh, gh], axis=1)
        for half in range(1, view):
            qn, gn = parts[half]
            packed = jnp.where(w == half, jnp.concatenate([qn, gn], axis=1), packed)
        qd_out[peer] = packed
    for oz in column:
        spot = {"pts": oz, "view": w}
        start(remote(qd_out.at[oz], qd.at[z], qd_s.at[oz], qd_r.at[z], spot))
    qd[z] = qd_out[z]

    for other, oz, ow in others:
        remote(meta.at[me], meta.at[other], meta_s.at[other], meta_r.at[other], {"pts": oz, "view": ow}).wait_recv()

    tile_of = lax.broadcasted_iota(jnp.int32, (META_ROWS, keys), 1) // (keys // (peers * (held // TILE)))
    for p in range(pts):
        hit = None
        for half in range(view):
            ids = meta[p * view + half]
            for i in range(nvis):
                one = ids[:, i : i + 1] == tile_of
                hit = one if hit is None else hit | one
        bias[p] = jnp.where(hit, 0.0, HIDDEN)
    row_number = lax.broadcasted_iota(jnp.int32, (pts * p_dev, WIDE), 0)
    for p in range(pts):
        for c in range(dest_rows):
            line = meta[p * view, qb_dev + c : qb_dev + c + 1, :]
            at = p * p_dev + c * WIDE
            place[:, at : at + WIDE] = jnp.where(row_number == line, 1.0, 0.0).astype(jnp.bfloat16)

    for other, oz, ow in others:
        remote(kv_out.at[0], kv.at[other], kv_s.at[other], kv_r.at[other], {"pts": oz, "view": ow}).wait_recv()
    grads[...] = jnp.zeros_like(grads)

    lower = lax.broadcasted_iota(jnp.int32, (p_dev, WIDE), 1) < DH
    zero = jnp.zeros((), jnp.bfloat16)
    scale = DH**-0.5
    nt = (((1,), (1,)), ((), ()))

    def shade(p):
        lines = [jnp.broadcast_to(bias[p, b : b + 1, :], (qblock, keys)) for b in range(qb_dev)]
        return jnp.concatenate(lines, axis=0)

    def block(p):
        both = kv[...].reshape(keys, WIDE)
        mixed = qd[p]
        query = jnp.where(lower, mixed * jnp.asarray(scale, jnp.bfloat16), zero)
        grad = jnp.where(lower, zero, mixed)
        scores = lax.dot_general(query, both, nt, preferred_element_type=jnp.float32)
        scores = scores + shade(p)
        d_prob = lax.dot_general(grad, both, nt, preferred_element_type=jnp.float32)
        peak = jnp.max(scores, axis=1, keepdims=True)
        weight = jnp.exp(scores - peak)
        total = jnp.sum(weight, axis=1, keepdims=True)
        inverse = 1.0 / total
        summed = jnp.dot(weight.astype(jnp.bfloat16), both, preferred_element_type=jnp.float32)
        out = (summed * inverse).astype(jnp.bfloat16)
        delta = jnp.sum(
            grad.astype(jnp.float32) * out.astype(jnp.float32), axis=1, keepdims=True
        )
        prob = weight * inverse
        d_score = (prob * (d_prob - delta)).astype(jnp.bfloat16)
        d_query = jnp.dot(d_score, both, preferred_element_type=jnp.float32) * scale
        left = jnp.concatenate([query, grad], axis=0)
        right = jnp.concatenate([d_score, prob.astype(jnp.bfloat16)], axis=0)
        grads[...] += jnp.dot(left.T, right, preferred_element_type=jnp.float32)
        return jnp.where(lower, d_query.astype(jnp.bfloat16), out)

    half_rows = p_dev // 2
    twin = {"pts": z, "view": lax.rem(w + 1, view)}

    def fold(upper, lower_half, side):
        at = slice(side * DH, (side + 1) * DH)
        return jnp.concatenate([upper[:, at], lower_half[:, at]], axis=1)

    def dq_copy(p):
        spot = {"pts": p, "view": w}
        return remote(dq_out.at[p], dq.at[me], dq_s.at[p], dq_r.at[me], spot)

    def twin_copy(source, target, sent, got, number):
        return remote(source, target.at[number], sent, got.at[number], twin)

    def step_body(step, carry):
        p = partner(z, step, pts)

        if step > 0:
            remote(qd_out.at[0], qd.at[p], qd_s.at[p], qd_r.at[p], {"pts": p, "view": w}).wait_recv()

        rows[p] = block(p)
        dq_out[p] = fold(rows[p, :half_rows, :], rows[p, half_rows:, :], 0)

        if step > 0:
            dq_copy(p).start()
        else:
            start(twin_copy(dq_out.at[z], dq, dq_s.at[z], dq_r, me))

        return carry

    for step in range(pts):
        step_body(step, 0)
    kept = []
    dq_own = pltpu.make_async_copy(dq_out.at[z], dq.at[me], load_s.at[0])
    dq_own.start()
    kept.append(dq_own)

    def send_att():
        every = rows[...].reshape(pts * p_dev, WIDE)
        moved = jnp.dot(place[...], every, preferred_element_type=jnp.float32)
        for p in range(pts):
            top = moved[p * p_dev : p * p_dev + half_rows]
            low = moved[p * p_dev + half_rows : (p + 1) * p_dev]
            att_out[p] = fold(top, low, 1).astype(jnp.bfloat16)
        for oz in column:
            spot = {"pts": oz, "view": w}
            start(remote(att_out.at[oz], att.at[me], att_s.at[oz], att_r.at[me], spot))
        start(twin_copy(att_out.at[z], att, att_s.at[z], att_r, me))
        att_own = pltpu.make_async_copy(att_out.at[z], att.at[me], load_s.at[1])
        att_own.start()
        kept.append(att_own)

    def send_dkv():
        dkv_out[...] = grads[...].T.astype(jnp.bfloat16).reshape(dkv_out.shape)
        for other, oz, ow in others:
            spot = {"pts": oz, "view": ow}
            start(remote(dkv_out.at[other], dkv.at[me], dkv_s.at[other], dkv_r.at[me], spot))
        dkv_own = pltpu.make_async_copy(dkv_out.at[me], dkv.at[me], load_s.at[2])
        dkv_own.start()
        kept.append(dkv_own)

    send_att()
    send_dkv()

    def arrived(buffer, sent, got, number):
        source = att_out.at[0] if buffer is not dkv else dkv_out.at[0]
        remote(source, buffer.at[number], sent.at[0], got.at[number], twin).wait_recv()

    for oz in column:
        number = oz * view + w
        arrived(dq, dq_s, dq_r, number)
        start(twin_copy(dq.at[number], dq, dq_s.at[pts + oz], dq_r, number))
    for oz in column:
        number = oz * view + w
        arrived(att, att_s, att_r, number)
        start(twin_copy(att.at[number], att, att_s.at[pts + oz], att_r, number))
    for other, _, _ in others:
        arrived(dkv, dkv_s, dkv_r, other)
    for oz in range(pts):
        number = oz * view + lax.rem(w + 1, view)
        arrived(dq, dq_s, dq_r, number)
        arrived(att, att_s, att_r, number)
    for oz in column:
        dq_copy(oz).wait_send()
    for copy in sends:
        copy.wait_send()
    for copy in kept:
        copy.wait()


def unpack_kernel(att, dq, dkv, att_hbm, dq_hbm, dk_hbm, dv_hbm, att_ref, dq_ref, dk_ref, dv_ref, sems):
    peers = att.shape[0]
    half_rows = att.shape[1]

    def write(source, target, number):
        copy = pltpu.make_async_copy(source, target, sems.at[number])
        copy.start()
        return copy

    def two(buffer, pair, side):
        at = slice(side * DH, (side + 1) * DH)
        return jnp.concatenate([buffer[2 * pair][:, at], buffer[2 * pair + 1][:, at]], axis=1)

    copies = []
    for number, (buffer, ref, out) in enumerate(((att, att_ref, att_hbm), (dq, dq_ref, dq_hbm))):
        for pair in range(peers // 2):
            cols = slice(pair * WIDE, (pair + 1) * WIDE)
            ref[:half_rows, cols] = two(buffer, pair, 0)
            ref[half_rows:, cols] = two(buffer, pair, 1)
        copies.append(write(ref, out, number))
    for side, (ref, out) in enumerate(((dk_ref, dk_hbm), (dv_ref, dv_hbm))):
        for pair in range(peers // 2):
            cols = slice(pair * WIDE, (pair + 1) * WIDE)
            ref[:, cols] = two(dkv, pair, side)
        copies.append(write(ref, out, 2 + side))
    for copy in copies:
        copy.wait()


def by_head(queries, key_tiles, value_tiles, visible, destination, d_out):
    pts = lax.axis_size("pts")
    view = lax.axis_size("view")
    peers = pts * view
    kv_dev, tile_keys, width = key_tiles.shape
    held = kv_dev * tile_keys
    p_dev = queries.shape[0]
    keys = peers * held
    whole = pl.BlockSpec(memory_space=pltpu.VMEM)
    bf = jnp.bfloat16
    dma = pltpu.SemaphoreType.DMA
    anywhere = pl.BlockSpec(memory_space=pltpu.HBM)
    vmem = pltpu.VMEM
    operands = (
        queries,
        key_tiles.reshape(held, width),
        value_tiles.reshape(held, width),
        visible,
        destination.reshape(p_dev // WIDE, WIDE),
        d_out,
    )
    landed = (
        jax.ShapeDtypeStruct((peers, p_dev // 2, WIDE), bf),
        jax.ShapeDtypeStruct((peers, p_dev // 2, WIDE), bf),
        jax.ShapeDtypeStruct((peers, held, WIDE), bf),
    )
    att, dq, dkv = pl.pallas_call(
        functools.partial(head_kernel, pts, view),
        out_shape=landed,
        in_specs=[anywhere] * 6,
        out_specs=(anywhere,) * 3,
        scratch_shapes=[vmem(x.shape, x.dtype) for x in operands]
        + [
            vmem((peers, META_ROWS, WIDE), jnp.int32),
            vmem((peers, held, WIDE), bf),
            vmem((peers, held, WIDE), bf),
            vmem((pts, p_dev, WIDE), bf),
            vmem((pts, p_dev, WIDE), bf),
            vmem((pts, META_ROWS, keys), jnp.float32),
            vmem((pts * p_dev, pts * p_dev), bf),
            vmem((pts, p_dev, WIDE), bf),
            vmem((WIDE, keys), jnp.float32),
            vmem((pts, p_dev // 2, WIDE), bf),
            vmem((pts, p_dev // 2, WIDE), bf),
            vmem((peers, held, WIDE), bf),
            dma((6,)),
            dma((peers,)),
            dma((peers,)),
            dma((peers,)),
            dma((peers,)),
            dma((pts,)),
            dma((pts,)),
            dma((2 * pts,)),
            dma((peers,)),
            dma((2 * pts,)),
            dma((peers,)),
            dma((peers,)),
            dma((peers,)),
        ],
        compiler_params=pltpu.CompilerParams(
            collective_id=0, has_side_effects=True, vmem_limit_bytes=ROOM
        ),
        cost_estimate=pl.CostEstimate(
            flops=14 * pts * p_dev * keys * DH,
            bytes_accessed=6 * p_dev * width * 2,
            transcendentals=pts * p_dev * keys,
        ),
    )(*operands)
    finals = [(p_dev, width), (p_dev, width), (held, width), (held, width)]
    attended, d_queries, d_keys, d_values = pl.pallas_call(
        unpack_kernel,
        out_shape=tuple(jax.ShapeDtypeStruct(shape, bf) for shape in finals),
        in_specs=[whole] * 3,
        out_specs=(anywhere,) * 4,
        scratch_shapes=[vmem(shape, bf) for shape in finals] + [dma((4,))],
    )(att, dq, dkv)
    return (
        attended,
        d_queries,
        d_keys.reshape(key_tiles.shape),
        d_values.reshape(value_tiles.shape),
    )


def solution(mesh):
    in_specs = (
        P(("scene", "pts"), "head"),
        P(("scene", "pts", "view"), None, "head"),
        P(("scene", "pts", "view"), None, "head"),
        P(("scene", "pts"), "view"),
        P(("scene", "pts")),
        P(("scene", "pts"), "head"),
    )
    out_specs = (
        P(("scene", "pts"), "head"),
        P(("scene", "pts"), "head"),
        P(("scene", "pts", "view"), None, "head"),
        P(("scene", "pts", "view"), None, "head"),
    )
    heads_local = HEADS // mesh.shape["head"]
    per_device = local
    pts = mesh.shape["pts"]
    paired = mesh.shape["view"] == 2 and pts & (pts - 1) == 0
    if paired and heads_local == pts * mesh.shape["view"]:
        per_device = by_head
    return jax.shard_map(per_device, mesh=mesh, in_specs=in_specs, out_specs=out_specs, check_vma=False)
```
